512 devices in a mesh: ga: 64 (over y, z_lo, x), col: 8 (over z_hi, core).
Axes of the slice: x: 4, y: 4, z: 16 (z_hi: 4, z_lo: 4; z = z_hi * 4 + z_lo), core: 2. Of those that a mesh axis runs over, the one named last changes fastest.
Arguments:
- valence: bfloat16 [128, 64, 4096], P('col', 'ga'), may hold values from -6 to 6
- conduction: bfloat16 [256, 64, 4096], P('col', 'ga'), may hold values from -6 to 6
- band_index: int32 [1], replicated, may hold values from 0 to 127
- occ_valence: int32 [128], replicated, may hold values from 1 to 2
- occ_conduction: int32 [256], P('col'), may hold values from 0 to 1
- gap_energy: float32 [256], P('col'), may hold values from 0.5 to 20
- row_map: int32 [8192], P('ga'), may hold values from 0 to 4095
- col_map: int32 [4096], P('ga'), may hold values from 0 to 4095
Outputs:
- chi_panel: float32 [2, 8192, 4096], P(None, 'ga', 'col')
The draws below stay inside these ranges and needn't reach their ends.
Inputs may be any that keep to these rules, and one draw needn't show every extreme that they name: `row_map`: maps give positions inside the slab of the row block that holds the entry; entries may repeat.
All inputs are finite; a program needn't handle non-finite values.
Results may differ from the reference program's by a relative error of at most 0.025.
Values may be sent and summed in bfloat16 or wider, within the bound.
No kernel may reach another device: no remote copies, remote signals or barrier semaphores. Data moves between devices by JAX's collectives and lax.ppermute only.
A program may use at most 64 MiB of HBM per device.

```python
import math
import jax
import jax.numpy as jnp
from jax import lax

NX = 64
NY = 64
NZ = 64
NC_DEV = 32
ROWS_DEV = 128
PANEL = 4096
NC = 256
NV = 128
ROWS = 8192
PANEL_DEV = 64
SLAB = 4096
N_GA = 64
N_COL = 8


def place_ends(entries, key, least, top_value):
    spot = [jax.random.randint(jax.random.fold_in(key, axis), (), 0, length) for axis, length in enumerate(entries.shape)]
    main_axis = entries.shape.index(max(entries.shape))
    beside = spot[:main_axis] + [(spot[main_axis] + 1) % entries.shape[main_axis]] + spot[main_axis + 1:]
    return entries.at[tuple(spot)].set(least).at[tuple(beside)].set(top_value)


def steps_of(own_key, extent, pieces, low, high):
    factor_of, own = 1.0, jax.random.fold_in(own_key, 6)
    for axis_at, shards_of in pieces:
        steps = jnp.exp(jax.random.uniform(jax.random.fold_in(own, axis_at), (shards_of,), jnp.float32, low / len(pieces), high / len(pieces)))
        factor_of = factor_of * jnp.repeat(steps, extent[axis_at] // shards_of).reshape([-1 if axis == axis_at else 1 for axis in range(len(extent))])
    return factor_of


def scatter_about(own_key, extent, scale, bound, shards=(), kind=jnp.bfloat16):
    array = jax.random.normal(own_key, extent, jnp.float32) * scale
    if len(shards) > 0:
        array = steps_of(own_key, extent, shards, -0.22, 0.18) * array
    return jnp.clip(array, min=-bound, max=bound).astype(kind)


def setup_inputs(seed: int = 0) -> dict:
    streams_of = jax.random.split(jax.random.key(seed), 9)
    valence = scatter_about(streams_of[0], (NV, NX, NY * NZ), 1.0, 6.0, ((0, 8), (1, 64)))
    conduction = scatter_about(streams_of[1], (NC, NX, NY * NZ), 1.0, 6.0, ((0, 8), (1, 64)))
    band_index = jax.random.randint(streams_of[2], (1,), 0, NV).astype(jnp.int32)
    occ_valence = place_ends(jax.random.randint(streams_of[3], (NV,), 1, 3), jax.random.fold_in(streams_of[3], 1), 1, 2).astype(jnp.int32)
    occ_conduction = place_ends(jax.random.randint(streams_of[4], (NC,), 0, 2), jax.random.fold_in(streams_of[4], 1), 0, 1).astype(jnp.int32)
    gap_energy = jnp.clip(jnp.exp(math.log(20.0) - 3.6888795 * jax.random.uniform(streams_of[5], (NC,), jnp.float32) ** steps_of(streams_of[5], (NC,), ((0, 8),), -0.2, 0.2)), 0.5, 20.0)
    row_map = place_ends(jax.random.randint(streams_of[6], (ROWS,), 0, SLAB), jax.random.fold_in(streams_of[6], 1), 0, SLAB - 1).astype(jnp.int32)
    col_map = place_ends(jax.random.randint(streams_of[7], (PANEL,), 0, SLAB), jax.random.fold_in(streams_of[7], 1), 0, SLAB - 1).astype(jnp.int32)
    return {"valence": valence, "conduction": conduction, "band_index": band_index, "occ_valence": occ_valence, "occ_conduction": occ_conduction, "gap_energy": gap_energy, "row_map": row_map, "col_map": col_map}


def rounded(values):
    return lax.optimization_barrier(values.astype(jnp.bfloat16)).astype(jnp.float32)

def flat_index(positions, owners):
    slab_rows = NY // N_GA
    freq_x = positions // (slab_rows * NZ)
    freq_y = owners * slab_rows + positions // NZ % slab_rows
    freq_z = positions % NZ
    return (freq_x * NY * NZ + freq_y * NZ + freq_z).astype(jnp.int32)

def reference(valence, conduction, band_index, occ_valence, occ_conduction, gap_energy, row_map, col_map):
    chosen = band_index[0]
    valence_band = lax.dynamic_index_in_dim(valence, chosen, 0, keepdims=False).astype(jnp.float32)
    occ_top = occ_valence[chosen]
    row_owner = jnp.arange(ROWS, dtype=jnp.int32) // ROWS_DEV
    row_index = flat_index(row_map, row_owner)
    col_order = col_map.reshape(N_GA, PANEL_DEV).T.reshape(-1)
    col_owner = jnp.arange(PANEL, dtype=jnp.int32) % N_GA
    col_index = flat_index(col_order, col_owner)
    total = jnp.zeros((2 * ROWS, PANEL), jnp.float32)
    for block in range(N_COL):
        lower = block * NC_DEV
        bands = conduction[lower:lower + NC_DEV].astype(jnp.float32)
        pair = rounded(valence_band[None] * bands).reshape(NC_DEV, NX, NY, NZ)
        first = jnp.fft.fft2(pair, axes=(2, 3), norm='ortho')
        mixed = rounded(jnp.real(first)) + 1j * rounded(jnp.imag(first))
        spectra = jnp.fft.fft(mixed, axis=1, norm='ortho').reshape(NC_DEV, -1)
        row_vals = spectra[:, row_index]
        col_vals = spectra[:, col_index]
        weight = 2.0 * (occ_conduction[lower:lower + NC_DEV] - occ_top).astype(jnp.float32) / gap_energy[lower:lower + NC_DEV]
        row_real = (jnp.real(row_vals).astype(jnp.float32) * weight[:, None]).T
        row_imag = (jnp.imag(row_vals).astype(jnp.float32) * weight[:, None]).T
        upper = jnp.concatenate([row_real, row_imag], axis=1)
        bottom = jnp.concatenate([row_imag, -row_real], axis=1)
        weighted = jnp.concatenate([upper, bottom], axis=0).astype(jnp.bfloat16)
        columns = jnp.concatenate([jnp.real(col_vals).astype(jnp.float32).T, jnp.imag(col_vals).astype(jnp.float32).T], axis=1).astype(jnp.bfloat16)
        total = total + rounded(jnp.dot(weighted, columns.T, preferred_element_type=jnp.float32))
    return total.reshape(2, ROWS, PANEL) * (1.0 / math.sqrt(NC))
```

```python
import math

import jax
import jax.numpy as jnp
import numpy as np
from jax import lax
from jax.experimental import pallas as pl
from jax.experimental.pallas import tpu as pltpu
from jax.sharding import Mesh
from jax.sharding import PartitionSpec as P

N = 64
BANDS = 32
ROWS = 128
COLS = 64
SPOTS = ROWS + COLS
LANES = 128
GA = ("y", "zl", "x")
COL = ("zh", "c")

f32 = jnp.float32
bf16 = jnp.bfloat16


def dot(left, right):
    return jnp.dot(left, right, preferred_element_type=f32)


def lane_index(shape):
    return lax.broadcasted_iota(jnp.int32, shape, len(shape) - 1)


def y_table():
    parity = np.arange(2)[:, None, None, None]
    ky = np.arange(N // 2)[None, :, None, None]
    imag = np.arange(2)[None, None, :, None]
    half = np.arange(N // 2)[None, None, None, :]
    turn = (ky * (2 * half + parity) + 16 * imag) % N
    return (np.cos(2.0 * np.pi * turn / N) / 8.0).reshape(LANES, N // 2).astype(np.float32)


def pair_y_kernel(v_ref, c_ref, e_ref, out_ref, by_band, by_ky):
    v = v_ref[...].astype(f32)
    for i in range(N // 2):
        bands = c_ref[:, i * LANES : (i + 1) * LANES].astype(f32)
        pair = (bands * v[i : i + 1, :]).astype(bf16).astype(f32)
        by_band[pl.ds(i, BANDS, stride=N // 2), :] = pair
    table = e_ref[...]
    low = lane_index((N, LANES)) < N
    for j in range(BANDS // 2):
        first = by_band[pl.ds(64 * j, 32), :]
        second = by_band[pl.ds(64 * j + 32, 32), :]
        both = dot(table, jnp.concatenate([first, second], axis=1).astype(bf16))
        even, odd = both[:N], both[N:]
        even = jnp.where(low, even[:, :LANES], pltpu.roll(even[:, LANES:], N, 1))
        odd = jnp.where(low, pltpu.roll(odd[:, :LANES], N, 1), odd[:, LANES:])
        by_ky[pl.ds(j, N, stride=16), :] = even + odd
        by_ky[pl.ds(1024 + j, N, stride=16), :] = even - odd
    out_ref[...] = by_ky[...].astype(bf16).reshape(N, 32, LANES)


def spots_kernel(r_ref, e_ref, pc_ref, ps_ref, w_ref, out_ref, planes):
    planes[...] = r_ref[...].reshape(N * 32, LANES).astype(f32)
    table = e_ref[...]
    cos_z = jnp.concatenate([pc_ref[...]] * 2, axis=1)
    sin_z = jnp.concatenate([ps_ref[...]] * 2, axis=1)
    column = lane_index((2 * LANES, LANES))
    band = lax.broadcasted_iota(jnp.int32, (2 * LANES, LANES), 0) // N
    total = jnp.zeros((2 * SPOTS, LANES), f32)
    for j in range(BANDS // 4):
        first = planes[pl.ds(2 * j, LANES, stride=16), :]
        second = planes[pl.ds(2 * j + 1, LANES, stride=16), :]
        at_x = dot(table, jnp.concatenate([first, second], axis=1).astype(bf16))
        real, imag = at_x[:SPOTS], at_x[SPOTS:]
        real_z = real * cos_z + imag * sin_z
        imag_z = imag * cos_z - real * sin_z
        terms = jnp.concatenate([real_z, imag_z], axis=0).astype(bf16)
        ones = jnp.where(column == band + 4 * j, 1.0, 0.0).astype(bf16)
        total = total + dot(terms, ones)
    joined = total[:SPOTS] + pltpu.roll(total[SPOTS:], BANDS, 1)
    joined = joined + pltpu.roll(joined, N, 1)
    out_ref[:ROWS, :] = (joined[:ROWS] * w_ref[0:1, :]).astype(bf16)
    out_ref[ROWS:, :] = (joined[ROWS:] * w_ref[1:2, :]).astype(bf16)


def panel_kernel(a_ref, b_ref, out_ref, spread, columns):
    spread[...] = b_ref[...].reshape(N * 32, LANES).astype(f32)
    for j in range(8):
        for q in range(4):
            columns[j * N : (j + 1) * N, q * LANES : (q + 1) * LANES] = spread[
                pl.ds(q * 8 + j, N, stride=32), :
            ].astype(bf16)
    real_lane = lane_index((ROWS, LANES)) % N < BANDS
    upper, lower = [], []
    for q in range(4):
        rows = a_ref[q, :ROWS, :]
        wide = rows.astype(f32)
        turned = jnp.where(
            real_lane, pltpu.roll(wide, LANES - BANDS, 1), -pltpu.roll(wide, BANDS, 1)
        )
        upper.append(rows)
        lower.append(turned.astype(bf16))
    both = jnp.concatenate(
        [jnp.concatenate(upper, axis=1), jnp.concatenate(lower, axis=1)], axis=0
    )
    for h in range(2):
        part = lax.dot_general(
            both,
            columns[h * 256 : (h + 1) * 256, :],
            (((1,), (1,)), ((), ())),
            preferred_element_type=f32,
        )
        part = part * (1.0 / 16.0)
        out_ref[0, :, h * 256 : (h + 1) * 256] = part[:ROWS]
        out_ref[1, :, h * 256 : (h + 1) * 256] = part[ROWS:]


def call(kernel, shape, dtype, scratch, *args):
    vmem = pl.BlockSpec(memory_space=pltpu.VMEM)
    return pl.pallas_call(
        kernel,
        out_shape=jax.ShapeDtypeStruct(shape, dtype),
        in_specs=[vmem] * len(args),
        out_specs=vmem,
        scratch_shapes=scratch,
        compiler_params=pltpu.CompilerParams(vmem_limit_bytes=32 * 1024 * 1024),
    )(*args)


def turns(count):
    return jnp.cos((count % N).astype(f32) * (2.0 * math.pi / N)) / 8.0


def shards(
    valence, conduction, band_index, occ_valence, occ_conduction, gap_energy, row_map, col_map
):
    chosen = band_index[0]
    core = lax.axis_index("c")
    mine = chosen // valence.shape[0] == lax.axis_index(COL)
    own = lax.dynamic_index_in_dim(valence, chosen % valence.shape[0], 0, keepdims=False)
    own = jnp.where(mine, own, 0).astype(bf16).reshape(32, LANES)
    v = lax.psum(lax.psum(own, "zh"), "c")

    half = call(
        pair_y_kernel,
        (N, 32, LANES),
        bf16,
        [pltpu.VMEM((1024, LANES), f32), pltpu.VMEM((2048, LANES), f32)],
        v,
        conduction.reshape(BANDS, N * N),
        jnp.asarray(y_table()).astype(bf16),
    )
    block = lax.all_to_all(half, GA, 0, 0, tiled=True)

    spots = jnp.concatenate([row_map, col_map])[:, None]
    kx, kz = spots // N, spots % N
    lane = lane_index((1, LANES))
    x, imag = lane // 2, lane % 2
    x_table = jnp.concatenate(
        [turns(kx * x + (N - 16) * imag), turns(kx * x + 16 * (1 - imag))], axis=0
    ).astype(bf16)
    z = lane % N
    cos_z, sin_z = turns(kz * z), turns(kz * z + N - 16)
    weight = 2.0 * (occ_conduction - occ_valence[chosen]).astype(f32) / gap_energy
    here = (lane // N == core).astype(f32)
    scales = jnp.concatenate([jnp.tile(weight, 4)[None] * here, here], axis=0)
    values = call(
        spots_kernel,
        (SPOTS, LANES),
        bf16,
        [pltpu.VMEM((2048, LANES), f32)],
        block,
        x_table,
        cos_z,
        sin_z,
        scales,
    )

    values = lax.psum(values, "c")
    rows = jnp.broadcast_to(values[None, :ROWS], (4, ROWS, LANES))
    cols = values[ROWS:].reshape(4, 16, LANES)
    bands = lax.all_to_all(jnp.concatenate([rows, cols], axis=1), "zh", 0, 0, tiled=True)
    own_cols = lax.dynamic_slice_in_dim(bands, ROWS + 8 * core, 8, axis=1).reshape(32, LANES)
    columns = lax.all_to_all(
        jnp.broadcast_to(own_cols[None], (N, 32, LANES)), GA, 0, 0, tiled=True
    )
    return call(
        panel_kernel,
        (2, ROWS, 8 * N),
        f32,
        [pltpu.VMEM((2048, LANES), f32), pltpu.VMEM((8 * N, 4 * LANES), bf16)],
        bands,
        columns,
    )


def solution(mesh):
    fine = Mesh(mesh.devices.reshape(4, 4, 4, 4, 2), ("y", "zl", "x", "zh", "c"))
    return jax.shard_map(
        shards,
        mesh=fine,
        in_specs=(
            P(COL, GA, None),
            P(COL, GA, None),
            P(),
            P(),
            P(COL),
            P(COL),
            P(GA),
            P(GA),
        ),
        out_specs=P(None, GA, COL),
        check_vma=False,
    )
```

```python
import math

import jax
import jax.numpy as jnp
import numpy as np
from jax import lax
from jax.experimental import pallas as pl
from jax.experimental.pallas import tpu as pltpu
from jax.sharding import Mesh
from jax.sharding import PartitionSpec as P

N = 64
BANDS = 32
ROWS = 128
COLS = 64
SPOTS = ROWS + COLS
LANES = 128
GA = ("y", "zl", "x")
COL = ("zh", "c")

f32 = jnp.float32
bf16 = jnp.bfloat16


def dot(left, right):
    return jnp.dot(left, right, preferred_element_type=f32)


def lane_index(shape):
    return lax.broadcasted_iota(jnp.int32, shape, len(shape) - 1)


def y_table():
    parity = np.arange(2)[:, None, None, None]
    ky = np.arange(N // 2)[None, :, None, None]
    imag = np.arange(2)[None, None, :, None]
    half = np.arange(N // 2)[None, None, None, :]
    turn = (ky * (2 * half + parity) + 16 * imag) % N
    return (np.cos(2.0 * np.pi * turn / N) / 8.0).reshape(LANES, N // 2).astype(np.float32)


def pair_y_kernel(v_ref, c_ref, e_ref, out_ref, by_band, by_ky):
    v = v_ref[...].astype(f32)
    for i in range(N // 2):
        bands = c_ref[:, i * LANES : (i + 1) * LANES].astype(f32)
        pair = (bands * v[i : i + 1, :]).astype(bf16).astype(f32)
        by_band[pl.ds(i, BANDS, stride=N // 2), :] = pair
    table = e_ref[...]
    low = lane_index((N, LANES)) < N
    for j in range(BANDS // 2):
        first = by_band[pl.ds(64 * j, 32), :]
        second = by_band[pl.ds(64 * j + 32, 32), :]
        both = dot(table, jnp.concatenate([first, second], axis=1).astype(bf16))
        even, odd = both[:N], both[N:]
        even = jnp.where(low, even[:, :LANES], pltpu.roll(even[:, LANES:], N, 1))
        odd = jnp.where(low, pltpu.roll(odd[:, :LANES], N, 1), odd[:, LANES:])
        by_ky[pl.ds(j, N, stride=16), :] = even + odd
        by_ky[pl.ds(1024 + j, N, stride=16), :] = even - odd
    out_ref[...] = by_ky[...].astype(bf16).reshape(N, 32, LANES)


def spots_kernel(r_ref, e_ref, pc_ref, ps_ref, w_ref, out_ref, planes):
    planes[...] = r_ref[...].reshape(N * 32, LANES).astype(f32)
    table = e_ref[...]
    cos_z = jnp.concatenate([pc_ref[...]] * 2, axis=1)
    sin_z = jnp.concatenate([ps_ref[...]] * 2, axis=1)
    column = lane_index((2 * LANES, LANES))
    band = lax.broadcasted_iota(jnp.int32, (2 * LANES, LANES), 0) // N
    total = jnp.zeros((2 * SPOTS, LANES), f32)
    for j in range(BANDS // 4):
        first = planes[pl.ds(2 * j, LANES, stride=16), :]
        second = planes[pl.ds(2 * j + 1, LANES, stride=16), :]
        at_x = dot(table, jnp.concatenate([first, second], axis=1).astype(bf16))
        real, imag = at_x[:SPOTS], at_x[SPOTS:]
        real_z = real * cos_z + imag * sin_z
        imag_z = imag * cos_z - real * sin_z
        terms = jnp.concatenate([real_z, imag_z], axis=0).astype(bf16)
        ones = jnp.where(column == band + 4 * j, 1.0, 0.0).astype(bf16)
        total = total + dot(terms, ones)
    joined = total[:SPOTS] + pltpu.roll(total[SPOTS:], BANDS, 1)
    rows = joined[:ROWS] * w_ref[0:1, :]
    rows = (rows[:N] + pltpu.roll(rows[N:], N, 1)).astype(bf16)
    cols = joined[ROWS:]
    cols = ((cols + pltpu.roll(cols, N, 1)) * w_ref[1:2, :]).astype(bf16)
    for q in range(4):
        out_ref[q, :N, :] = rows
        out_ref[q, N:, :] = cols[16 * q : 16 * q + 16]


def panel_kernel(a_ref, b_ref, out_ref, spread, columns):
    spread[...] = b_ref[...].reshape(N * 32, LANES).astype(f32)
    for j in range(8):
        for q in range(4):
            columns[j * N : (j + 1) * N, q * LANES : (q + 1) * LANES] = spread[
                pl.ds(q * 8 + j, N, stride=32), :
            ].astype(bf16)
    real_lane = lane_index((ROWS, LANES)) % N < BANDS
    upper, lower = [], []
    low = lane_index((N, LANES)) < N
    for q in range(4):
        core0 = a_ref[0, q, :N, :].astype(f32)
        core1 = a_ref[1, q, :N, :].astype(f32)
        head = jnp.where(low, core0, pltpu.roll(core1, N, 1))
        tail = jnp.where(low, pltpu.roll(core0, N, 1), core1)
        rows = jnp.concatenate([head, tail], axis=0)
        turned = jnp.where(
            real_lane, pltpu.roll(rows, LANES - BANDS, 1), -pltpu.roll(rows, BANDS, 1)
        )
        upper.append(rows.astype(bf16))
        lower.append(turned.astype(bf16))
    both = jnp.concatenate(
        [jnp.concatenate(upper, axis=1), jnp.concatenate(lower, axis=1)], axis=0
    )
    for h in range(2):
        part = lax.dot_general(
            both,
            columns[h * 256 : (h + 1) * 256, :],
            (((1,), (1,)), ((), ())),
            preferred_element_type=f32,
        )
        part = part * (1.0 / 16.0)
        out_ref[0, :, h * 256 : (h + 1) * 256] = part[:ROWS]
        out_ref[1, :, h * 256 : (h + 1) * 256] = part[ROWS:]


def call(kernel, shape, dtype, scratch, *args):
    vmem = pl.BlockSpec(memory_space=pltpu.VMEM)
    return pl.pallas_call(
        kernel,
        out_shape=jax.ShapeDtypeStruct(shape, dtype),
        in_specs=[vmem] * len(args),
        out_specs=vmem,
        scratch_shapes=scratch,
        compiler_params=pltpu.CompilerParams(vmem_limit_bytes=32 * 1024 * 1024),
    )(*args)


def turns(count):
    return jnp.cos((count % N).astype(f32) * (2.0 * math.pi / N)) / 8.0


def shards(
    valence, conduction, band_index, occ_valence, occ_conduction, gap_energy, row_map, col_map
):
    chosen = band_index[0]
    core = lax.axis_index("c")
    mine = chosen // valence.shape[0] == lax.axis_index(COL)
    own = lax.dynamic_index_in_dim(valence, chosen % valence.shape[0], 0, keepdims=False)
    own = jnp.where(mine, own, 0).astype(bf16).reshape(32, LANES)
    v = lax.psum(lax.psum(own, "zh"), "c")

    half = call(
        pair_y_kernel,
        (N, 32, LANES),
        bf16,
        [pltpu.VMEM((1024, LANES), f32), pltpu.VMEM((2048, LANES), f32)],
        v,
        conduction.reshape(BANDS, N * N),
        jnp.asarray(y_table()).astype(bf16),
    )
    block = lax.all_to_all(half, GA, 0, 0, tiled=True)

    spots = jnp.concatenate([row_map, col_map])[:, None]
    kx, kz = spots // N, spots % N
    lane = lane_index((1, LANES))
    x, imag = lane // 2, lane % 2
    x_table = jnp.concatenate(
        [turns(kx * x + (N - 16) * imag), turns(kx * x + 16 * (1 - imag))], axis=0
    ).astype(bf16)
    z = lane % N
    cos_z, sin_z = turns(kz * z), turns(kz * z + N - 16)
    weight = 2.0 * (occ_conduction - occ_valence[chosen]).astype(f32) / gap_energy
    here = (lane // N == core).astype(f32)
    scales = jnp.concatenate([jnp.tile(weight, 4)[None], here], axis=0)
    values = call(
        spots_kernel,
        (4, N + 16, LANES),
        bf16,
        [pltpu.VMEM((2048, LANES), f32)],
        block,
        x_table,
        cos_z,
        sin_z,
        scales,
    )

    values = lax.all_to_all(values, "zh", 0, 0, tiled=True)
    bands = lax.all_gather(values, "c")
    own_cols = lax.dynamic_slice_in_dim(bands, N + 8 * core, 8, axis=2)
    own_cols = (own_cols[0] + own_cols[1]).reshape(32, LANES)
    columns = lax.all_to_all(
        jnp.broadcast_to(own_cols[None], (N, 32, LANES)), GA, 0, 0, tiled=True
    )
    return call(
        panel_kernel,
        (2, ROWS, 8 * N),
        f32,
        [pltpu.VMEM((2048, LANES), f32), pltpu.VMEM((8 * N, 4 * LANES), bf16)],
        bands,
        columns,
    )


def solution(mesh):
    fine = Mesh(mesh.devices.reshape(4, 4, 4, 4, 2), ("y", "zl", "x", "zh", "c"))
    return jax.shard_map(
        shards,
        mesh=fine,
        in_specs=(
            P(COL, GA, None),
            P(COL, GA, None),
            P(),
            P(),
            P(COL),
            P(COL),
            P(GA),
            P(GA),
        ),
        out_specs=P(None, GA, COL),
        check_vma=False,
    )
```

```python
import math

import jax
import jax.numpy as jnp
import numpy as np
from jax import lax
from jax.experimental import pallas as pl
from jax.experimental.pallas import tpu as pltpu
from jax.sharding import Mesh
from jax.sharding import PartitionSpec as P

N = 64
BANDS = 32
ROWS = 128
COLS = 64
SPOTS = ROWS + COLS
LANES = 128
WIDE = 40
NARROW = 24
GA = ("y", "zl", "x")
COL = ("zh", "c")

f32 = jnp.float32
bf16 = jnp.bfloat16


def dot(left, right):
    return jnp.dot(left, right, preferred_element_type=f32)


def lane_index(shape):
    return lax.broadcasted_iota(jnp.int32, shape, len(shape) - 1)


def y_table():
    parity = np.arange(2)[:, None, None, None]
    ky = np.arange(N // 2)[None, :, None, None]
    imag = np.arange(2)[None, None, :, None]
    half = np.arange(N // 2)[None, None, None, :]
    turn = (ky * (2 * half + parity) + 16 * imag) % N
    return (np.cos(2.0 * np.pi * turn / N) / 8.0).reshape(LANES, N // 2).astype(np.float32)


def pair_y_kernel(v_ref, c_ref, e_ref, out_ref, by_band, by_ky):
    v = v_ref[...].astype(f32)
    for i in range(N // 2):
        bands = c_ref[:, i * LANES : (i + 1) * LANES].astype(f32)
        pair = (bands * v[i : i + 1, :]).astype(bf16).astype(f32)
        by_band[pl.ds(i, BANDS, stride=WIDE), :] = pair
    table = e_ref[...]
    low = lane_index((N, LANES)) < N
    for j in range(BANDS // 2):
        first = by_band[pl.ds(2 * WIDE * j, 32), :]
        second = by_band[pl.ds(2 * WIDE * j + WIDE, 32), :]
        both = dot(table, jnp.concatenate([first, second], axis=1).astype(bf16))
        even, odd = both[:N], both[N:]
        even = jnp.where(low, even[:, :LANES], pltpu.roll(even[:, LANES:], N, 1))
        odd = jnp.where(low, pltpu.roll(odd[:, :LANES], N, 1), odd[:, LANES:])
        by_ky[pl.ds(j, N, stride=NARROW), :] = even + odd
        by_ky[pl.ds(N * NARROW + j, N, stride=NARROW), :] = even - odd
    for ky in range(N):
        real = by_ky[pl.ds(2 * ky * NARROW, 16), :]
        imag = by_ky[pl.ds((2 * ky + 1) * NARROW, 16), :]
        out_ref[ky] = jnp.concatenate([real, imag], axis=0).astype(bf16)


def spots_kernel(r_ref, e_ref, pc_ref, ps_ref, w_ref, out_ref, planes):
    planes[...] = r_ref[...].reshape(N * 32, LANES).astype(f32)
    table = e_ref[...]
    cos_z = jnp.concatenate([pc_ref[...]] * 2, axis=1)
    sin_z = jnp.concatenate([ps_ref[...]] * 2, axis=1)
    column = lane_index((2 * LANES, LANES))
    band = lax.broadcasted_iota(jnp.int32, (2 * LANES, LANES), 0) // N
    total = jnp.zeros((2 * SPOTS, LANES), f32)
    for j in range(BANDS // 4):
        first = planes[pl.ds(2 * j, LANES, stride=16), :]
        second = planes[pl.ds(2 * j + 1, LANES, stride=16), :]
        at_x = dot(table, jnp.concatenate([first, second], axis=1).astype(bf16))
        real, imag = at_x[:SPOTS], at_x[SPOTS:]
        real_z = real * cos_z + imag * sin_z
        imag_z = imag * cos_z - real * sin_z
        terms = jnp.concatenate([real_z, imag_z], axis=0).astype(bf16)
        ones = jnp.where(column == band + 4 * j, 1.0, 0.0).astype(bf16)
        total = total + dot(terms, ones)
    joined = total[:SPOTS] + pltpu.roll(total[SPOTS:], BANDS, 1)
    rows = joined[:ROWS] * w_ref[0:1, :]
    rows = (rows[:N] + pltpu.roll(rows[N:], N, 1)).astype(bf16)
    cols = joined[ROWS:]
    cols = ((cols + pltpu.roll(cols, N, 1)) * w_ref[1:2, :]).astype(bf16)
    for q in range(4):
        out_ref[q, :N, :] = rows
        out_ref[q, N:, :] = cols[16 * q : 16 * q + 16]


def panel_kernel(a_ref, b_ref, out_ref, spread):
    for y in range(4):
        for x in range(4):
            for zl in range(4):
                at = (16 * y + 4 * zl + x) * WIDE
                spread[pl.ds(at, 32), :] = b_ref[4 * y + x, 32 * zl : 32 * zl + 32, :].astype(f32)
    real_lane = lane_index((ROWS, LANES)) % N < BANDS
    upper, lower = [], []
    low = lane_index((N, LANES)) < N
    for q in range(4):
        core0 = a_ref[0, q, :N, :].astype(f32)
        core1 = a_ref[1, q, :N, :].astype(f32)
        head = jnp.where(low, core0, pltpu.roll(core1, N, 1))
        tail = jnp.where(low, pltpu.roll(core0, N, 1), core1)
        rows = jnp.concatenate([head, tail], axis=0)
        turned = jnp.where(
            real_lane, pltpu.roll(rows, LANES - BANDS, 1), -pltpu.roll(rows, BANDS, 1)
        )
        upper.append(rows.astype(bf16))
        lower.append(turned.astype(bf16))
    both = jnp.concatenate(
        [jnp.concatenate(upper, axis=1), jnp.concatenate(lower, axis=1)], axis=0
    )
    for h in range(2):
        columns = []
        for j in range(4 * h, 4 * h + 4):
            parts = [spread[pl.ds(8 * q + j, N, stride=WIDE), :] for q in range(4)]
            columns.append(jnp.concatenate(parts, axis=1))
        part = lax.dot_general(
            both,
            jnp.concatenate(columns, axis=0).astype(bf16),
            (((1,), (1,)), ((), ())),
            preferred_element_type=f32,
        )
        part = part * (1.0 / 16.0)
        out_ref[0, :, h * 256 : (h + 1) * 256] = part[:ROWS]
        out_ref[1, :, h * 256 : (h + 1) * 256] = part[ROWS:]


def call(kernel, shape, dtype, scratch, *args):
    vmem = pl.BlockSpec(memory_space=pltpu.VMEM)
    return pl.pallas_call(
        kernel,
        out_shape=jax.ShapeDtypeStruct(shape, dtype),
        in_specs=[vmem] * len(args),
        out_specs=vmem,
        scratch_shapes=scratch,
        compiler_params=pltpu.CompilerParams(vmem_limit_bytes=32 * 1024 * 1024),
    )(*args)


def turns(count):
    return jnp.cos((count % N).astype(f32) * (2.0 * math.pi / N)) / 8.0


def shards(
    valence, conduction, band_index, occ_valence, occ_conduction, gap_energy, row_map, col_map
):
    chosen = band_index[0]
    core = lax.axis_index("c")
    mine = chosen // valence.shape[0] == lax.axis_index(COL)
    own = lax.dynamic_index_in_dim(valence, chosen % valence.shape[0], 0, keepdims=False)
    own = jnp.where(mine, own, 0).astype(bf16).reshape(32, LANES)
    v = lax.psum(lax.psum(own, "c"), "zh")

    half = call(
        pair_y_kernel,
        (N, 32, LANES),
        bf16,
        [pltpu.VMEM((BANDS * WIDE, LANES), f32), pltpu.VMEM((2 * N * NARROW, LANES), f32)],
        v,
        conduction.reshape(BANDS, N * N),
        jnp.asarray(y_table()).astype(bf16),
    )
    block = lax.all_to_all(half, GA, 0, 0, tiled=True)

    spots = jnp.concatenate([row_map, col_map])[:, None]
    kx, kz = spots // N, spots % N
    lane = lane_index((1, LANES))
    x, imag = lane // 2, lane % 2
    x_table = jnp.concatenate(
        [turns(kx * x + (N - 16) * imag), turns(kx * x + 16 * (1 - imag))], axis=0
    ).astype(bf16)
    z = lane % N
    cos_z, sin_z = turns(kz * z), turns(kz * z + N - 16)
    weight = 2.0 * (occ_conduction - occ_valence[chosen]).astype(f32) / gap_energy
    here = (lane // N == core).astype(f32)
    scales = jnp.concatenate([jnp.tile(weight, 4)[None], here], axis=0)
    values = call(
        spots_kernel,
        (4, N + 16, LANES),
        bf16,
        [pltpu.VMEM((2048, LANES), f32)],
        block,
        x_table,
        cos_z,
        sin_z,
        scales,
    )

    values = lax.all_to_all(values, "zh", 0, 0, tiled=True)
    bands = lax.all_gather(values, "c")
    cols = values[:, N:, :].reshape(4, 2, 8, LANES).transpose(1, 0, 2, 3)
    cols = jnp.broadcast_to(cols[None], (4, 2, 4, 8, LANES)).reshape(8, 32, LANES)
    cols = lax.all_to_all(cols, ("zl", "c"), 0, 0, tiled=True).reshape(4, 2, 32, LANES)
    cols = (cols[:, 0] + cols[:, 1]).reshape(1, ROWS, LANES)
    columns = lax.all_to_all(
        jnp.broadcast_to(cols, (16, ROWS, LANES)), ("y", "x"), 0, 0, tiled=True
    )
    return call(
        panel_kernel,
        (2, ROWS, 8 * N),
        f32,
        [pltpu.VMEM((N * WIDE, LANES), f32)],
        bands,
        columns,
    )


def solution(mesh):
    fine = Mesh(mesh.devices.reshape(4, 4, 4, 4, 2), ("y", "zl", "x", "zh", "c"))
    return jax.shard_map(
        shards,
        mesh=fine,
        in_specs=(
            P(COL, GA, None),
            P(COL, GA, None),
            P(),
            P(),
            P(COL),
            P(COL),
            P(GA),
            P(GA),
        ),
        out_specs=P(None, GA, COL),
        check_vma=False,
    )
```

```python
import math

import jax
import jax.numpy as jnp
import numpy as np
from jax import lax
from jax.experimental import pallas as pl
from jax.experimental.pallas import tpu as pltpu
from jax.sharding import Mesh
from jax.sharding import PartitionSpec as P

N = 64
BANDS = 32
ROWS = 128
COLS = 64
SPOTS = ROWS + COLS
LANES = 128
WIDE = 40
NARROW = 24
PARTS = 4
GA = ("y", "zl", "x")
COL = ("zh", "c")

f32 = jnp.float32
bf16 = jnp.bfloat16


def dot(left, right):
    return jnp.dot(left, right, preferred_element_type=f32)


def lane_index(shape):
    return lax.broadcasted_iota(jnp.int32, shape, len(shape) - 1)


def y_table():
    parity = np.arange(2)[:, None, None, None]
    ky = np.arange(N // 2)[None, :, None, None]
    imag = np.arange(2)[None, None, :, None]
    half = np.arange(N // 2)[None, None, None, :]
    turn = (ky * (2 * half + parity) + 16 * imag) % N
    return (np.cos(2.0 * np.pi * turn / N) / 8.0).reshape(LANES, N // 2).astype(np.float32)


def pair_y_kernel(v_ref, c_ref, e_ref, out_ref, by_band, by_ky):
    v = v_ref[...].astype(f32)
    for i in range(N // 2):
        bands = c_ref[:, i * LANES : (i + 1) * LANES].astype(f32)
        pair = (bands * v[i : i + 1, :]).astype(bf16).astype(f32)
        by_band[pl.ds(i, BANDS, stride=WIDE), :] = pair
    table = e_ref[...]
    low = lane_index((N, LANES)) < N
    for j in range(BANDS // 2):
        first = by_band[pl.ds(2 * WIDE * j, 32), :]
        second = by_band[pl.ds(2 * WIDE * j + WIDE, 32), :]
        both = dot(table, jnp.concatenate([first, second], axis=1).astype(bf16))
        even, odd = both[:N], both[N:]
        even = jnp.where(low, even[:, :LANES], pltpu.roll(even[:, LANES:], N, 1))
        odd = jnp.where(low, pltpu.roll(odd[:, :LANES], N, 1), odd[:, LANES:])
        by_ky[pl.ds(j, N, stride=NARROW), :] = even + odd
        by_ky[pl.ds(N * NARROW + j, N, stride=NARROW), :] = even - odd
    for ky in range(N):
        real = by_ky[pl.ds(2 * ky * NARROW, 16), :]
        imag = by_ky[pl.ds((2 * ky + 1) * NARROW, 16), :]
        out_ref[ky] = jnp.concatenate([real, imag], axis=0).astype(bf16)


def spots_kernel(r_ref, e_ref, pc_ref, ps_ref, w_ref, out_ref, planes):
    planes[...] = r_ref[...].reshape(N * 32, LANES).astype(f32)
    table = e_ref[...]
    cos_z = jnp.concatenate([pc_ref[...]] * 2, axis=1)
    sin_z = jnp.concatenate([ps_ref[...]] * 2, axis=1)
    column = lane_index((2 * LANES, LANES))
    band = lax.broadcasted_iota(jnp.int32, (2 * LANES, LANES), 0) // N
    total = jnp.zeros((2 * SPOTS, LANES), f32)
    for j in range(BANDS // 4):
        first = planes[pl.ds(2 * j, LANES, stride=16), :]
        second = planes[pl.ds(2 * j + 1, LANES, stride=16), :]
        at_x = dot(table, jnp.concatenate([first, second], axis=1).astype(bf16))
        real, imag = at_x[:SPOTS], at_x[SPOTS:]
        real_z = real * cos_z + imag * sin_z
        imag_z = imag * cos_z - real * sin_z
        terms = jnp.concatenate([real_z, imag_z], axis=0).astype(bf16)
        ones = jnp.where(column == band + 4 * j, 1.0, 0.0).astype(bf16)
        total = total + dot(terms, ones)
    joined = total[:SPOTS] + pltpu.roll(total[SPOTS:], BANDS, 1)
    rows = joined[:ROWS] * w_ref[0:1, :]
    rows = (rows[:N] + pltpu.roll(rows[N:], N, 1)).astype(bf16)
    cols = joined[ROWS:]
    cols = ((cols + pltpu.roll(cols, N, 1)) * w_ref[1:2, :]).astype(bf16)
    for q in range(4):
        out_ref[q, :N, :] = rows
        out_ref[q, N:, :] = cols[16 * q : 16 * q + 16]


def panel_kernel(a_ref, b_ref, out_ref, spread):
    for y in range(4):
        for x in range(4):
            for zl in range(4):
                at = (16 * y + 4 * zl + x) * WIDE
                spread[pl.ds(at, 32), :] = b_ref[4 * y + x, 32 * zl : 32 * zl + 32, :].astype(f32)
    real_lane = lane_index((ROWS, LANES)) % N < BANDS
    upper, lower = [], []
    low = lane_index((N, LANES)) < N
    for q in range(4):
        core0 = a_ref[0, q, :N, :].astype(f32)
        core1 = a_ref[1, q, :N, :].astype(f32)
        head = jnp.where(low, core0, pltpu.roll(core1, N, 1))
        tail = jnp.where(low, pltpu.roll(core0, N, 1), core1)
        rows = jnp.concatenate([head, tail], axis=0)
        turned = jnp.where(
            real_lane, pltpu.roll(rows, LANES - BANDS, 1), -pltpu.roll(rows, BANDS, 1)
        )
        upper.append(rows.astype(bf16))
        lower.append(turned.astype(bf16))
    both = jnp.concatenate(
        [jnp.concatenate(upper, axis=1), jnp.concatenate(lower, axis=1)], axis=0
    )
    for h in range(2):
        columns = []
        for j in range(4 * h, 4 * h + 4):
            parts = [spread[pl.ds(8 * q + j, N, stride=WIDE), :] for q in range(4)]
            columns.append(jnp.concatenate(parts, axis=1))
        part = lax.dot_general(
            both,
            jnp.concatenate(columns, axis=0).astype(bf16),
            (((1,), (1,)), ((), ())),
            preferred_element_type=f32,
        )
        part = part * (1.0 / 16.0)
        out_ref[0, :, h * 256 : (h + 1) * 256] = part[:ROWS]
        out_ref[1, :, h * 256 : (h + 1) * 256] = part[ROWS:]


def call(kernel, shape, dtype, scratch, *args, in_hbm=()):
    vmem = pl.BlockSpec(memory_space=pltpu.VMEM)
    hbm = pl.BlockSpec(memory_space=pltpu.HBM)
    return pl.pallas_call(
        kernel,
        out_shape=jax.ShapeDtypeStruct(shape, dtype),
        in_specs=[hbm if i in in_hbm else vmem for i in range(len(args))],
        out_specs=vmem,
        scratch_shapes=scratch,
        compiler_params=pltpu.CompilerParams(vmem_limit_bytes=32 * 1024 * 1024),
    )(*args)


def turns(count):
    return jnp.cos((count % N).astype(f32) * (2.0 * math.pi / N)) / 8.0


def shards(
    valence, conduction, band_index, occ_valence, occ_conduction, gap_energy, row_map, col_map
):
    chosen = band_index[0]
    core = lax.axis_index("c")
    mine = chosen // valence.shape[0] == lax.axis_index(COL)
    own = lax.dynamic_index_in_dim(valence, chosen % valence.shape[0], 0, keepdims=False)
    own = jnp.where(mine, own, 0).astype(bf16).reshape(32, LANES)
    both = lax.all_gather(own, "c")
    v = lax.psum(both[0] + both[1], "zh")

    half = call(
        pair_y_kernel,
        (N, 32, LANES),
        bf16,
        [
            pltpu.VMEM((BANDS * WIDE, LANES), f32),
            pltpu.VMEM((2 * N * NARROW, LANES), f32),
        ],
        v,
        conduction.reshape(BANDS, N * N),
        jnp.asarray(y_table()).astype(bf16),
    )
    block = lax.all_to_all(half, GA, 0, 0, tiled=True)

    spots = jnp.concatenate([row_map, col_map])[:, None]
    kx, kz = spots // N, spots % N
    lane = lane_index((1, LANES))
    x, imag = lane // 2, lane % 2
    x_table = jnp.concatenate(
        [turns(kx * x + (N - 16) * imag), turns(kx * x + 16 * (1 - imag))], axis=0
    ).astype(bf16)
    z = lane % N
    cos_z, sin_z = turns(kz * z), turns(kz * z + N - 16)
    weight = 2.0 * (occ_conduction - occ_valence[chosen]).astype(f32) / gap_energy
    here = (lane // N == core).astype(f32)
    scales = jnp.concatenate([jnp.tile(weight, 4)[None], here], axis=0)
    values = call(
        spots_kernel,
        (4, N + 16, LANES),
        bf16,
        [pltpu.VMEM((2048, LANES), f32)],
        block,
        x_table,
        cos_z,
        sin_z,
        scales,
    )

    values = lax.all_to_all(values, "zh", 0, 0, tiled=True)
    bands = lax.all_gather(values, "c")
    cols = values[:, N:, :].reshape(4, 2, 8, LANES).transpose(1, 0, 2, 3)
    cols = jnp.broadcast_to(cols[None], (4, 2, 4, 8, LANES)).reshape(8, 32, LANES)
    cols = lax.all_to_all(cols, ("zl", "c"), 0, 0, tiled=True).reshape(4, 2, 32, LANES)
    cols = (cols[:, 0] + cols[:, 1]).reshape(1, ROWS, LANES)
    cols, bands = lax.optimization_barrier((cols, bands))
    columns = lax.all_to_all(
        jnp.broadcast_to(cols, (16, ROWS, LANES)), ("y", "x"), 0, 0, tiled=True
    )
    return call(
        panel_kernel,
        (2, ROWS, 8 * N),
        f32,
        [pltpu.VMEM((N * WIDE, LANES), f32)],
        bands,
        columns,
    )


def solution(mesh):
    fine = Mesh(mesh.devices.reshape(4, 4, 4, 4, 2), ("y", "zl", "x", "zh", "c"))
    return jax.shard_map(
        shards,
        mesh=fine,
        in_specs=(
            P(COL, GA, None),
            P(COL, GA, None),
            P(),
            P(),
            P(COL),
            P(COL),
            P(GA),
            P(GA),
        ),
        out_specs=P(None, GA, COL),
        check_vma=False,
    )
```

```python
import jax
import jax.numpy as jnp
import numpy as np
from jax import lax
from jax.experimental import pallas as pl
from jax.experimental.pallas import tpu as pltpu
from jax.sharding import Mesh
from jax.sharding import PartitionSpec as P

N = 64
BANDS = 32
ROWS = 128
COLS = 64
SPOTS = ROWS + COLS
LANES = 128
WIDE = 40
PARTS = 4
GA = ("y", "zl", "x")
COL = ("zh", "c")

f32 = jnp.float32
bf16 = jnp.bfloat16


def dot(left, right):
    return jnp.dot(left, right, preferred_element_type=f32)


def lane_index(shape):
    return lax.broadcasted_iota(jnp.int32, shape, len(shape) - 1)


def y_table():
    parity = np.arange(2)[:, None, None, None]
    imag = np.arange(2)[None, :, None, None]
    ky = np.arange(N // 2)[None, None, :, None]
    half = np.arange(N // 2)[None, None, None, :]
    turn = (ky * (2 * half + parity) + 16 * imag) % N
    return wave(turn).reshape(LANES, N // 2)


def wave(turn):
    return (np.cos(2.0 * np.pi * (turn % N) / N) / 8.0).astype(np.float32)


def x_table():
    kx = np.arange(N)[:, None]
    lane = np.arange(LANES)[None, :]
    plane, imag = lane // 8, lane // 4 % 2
    x = 16 * (plane // 4) + 4 * (lane % 4) + plane % 4
    return np.concatenate([wave(kx * x - 16 * imag), wave(kx * x + 16 * (1 - imag))], axis=1)


def z_table():
    turn = np.arange(N)[:, None] * (np.arange(LANES)[None, :] % N)
    return np.concatenate([wave(turn), wave(turn - 16)], axis=1)


def pair_kernel(v_ref, c_ref, row_ref, col_ref, out_ref):
    v = v_ref[...].astype(f32)
    for i in range(N // 2):
        lanes = pl.ds(i * LANES, LANES)
        out_ref[:, lanes] = (c_ref[:, lanes].astype(f32) * v[i : i + 1, :]).astype(bf16)
    row = row_ref[...]
    col = jnp.concatenate([col_ref[...]] * 2, axis=1)
    spots = [row >> 6, row & (N - 1), col >> 6, col & (N - 1)]
    spots = jnp.concatenate(spots * 2, axis=0).astype(f32)
    out_ref[:, N * N :] = jnp.concatenate([spots] * 4, axis=0).astype(bf16)


def y_kernel(p_ref, e_ref, out_ref, by_row, by_ky):
    for i in range(N // 2):
        by_row[pl.ds(i, BANDS, stride=WIDE), :] = p_ref[:, i * LANES : (i + 1) * LANES].astype(f32)
    table = e_ref[...]
    low = lane_index((N, LANES)) < N
    half = N // 2
    for j in range(BANDS // 2):
        first = by_row[pl.ds(2 * WIDE * j, half), :]
        second = by_row[pl.ds(2 * WIDE * j + WIDE, half), :]
        both = dot(table, jnp.concatenate([first, second], axis=1).astype(bf16))
        even, odd = both[:N], both[N:]
        even = jnp.where(low, even[:, :LANES], pltpu.roll(even[:, LANES:], N, 1))
        odd = jnp.where(low, pltpu.roll(odd[:, :LANES], N, 1), odd[:, LANES:])
        at = 8 * (j % 4) + j // 4
        for start, value in ((at, even + odd), (half * WIDE + at, even - odd)):
            by_ky[pl.ds(start, half, stride=WIDE), :] = value[:half]
            by_ky[pl.ds(start + 4, half, stride=WIDE), :] = value[half:]
    for ky in range(N):
        y, zl, x = ky // 16, ky // 4 % 4, ky % 4
        out_ref[4 * y + x, 32 * zl : 32 * zl + 32, :] = by_ky[pl.ds(ky * WIDE, 32), :].astype(bf16)


def spots_kernel(r_ref, e_ref, p_ref, w_ref, out_ref):
    column = lane_index((2 * LANES, LANES))
    band = lax.broadcasted_iota(jnp.int32, (2 * LANES, LANES), 0) // N
    total = jnp.zeros((2 * SPOTS, LANES), f32)
    for g in range(4):
        planes = r_ref[:, 32 * g : 32 * g + 32, :].astype(f32)
        table = jnp.concatenate([e_ref[g, :, :LANES], e_ref[g, :, LANES:]], axis=0)
        cos_z = jnp.concatenate([p_ref[g, :, :LANES].astype(f32)] * 2, axis=1)
        sin_z = jnp.concatenate([p_ref[g, :, LANES:].astype(f32)] * 2, axis=1)
        for h in range(2):
            first = planes[:, 16 * h : 16 * h + 8, :].reshape(LANES, LANES)
            second = planes[:, 16 * h + 8 : 16 * h + 16, :].reshape(LANES, LANES)
            at_x = dot(table, jnp.concatenate([first, second], axis=1).astype(bf16))
            real, imag = at_x[:SPOTS], at_x[SPOTS:]
            real_z = real * cos_z + imag * sin_z
            imag_z = imag * cos_z - real * sin_z
            terms = jnp.concatenate([real_z, imag_z], axis=0).astype(bf16)
            ones = jnp.where(column == band + 16 * g + 4 * h, 1.0, 0.0).astype(bf16)
            total = total + dot(terms, ones)
    joined = total[:SPOTS] + pltpu.roll(total[SPOTS:], 8, 1)
    rows = (joined[:ROWS] * w_ref[...]).T
    for q in range(4):
        cols = joined[ROWS + 16 * q : ROWS + 16 * q + 16]
        cols = cols[:8] + pltpu.roll(cols[8:], N, 1)
        for g in range(4):
            block = [rows[16 * g : 16 * g + 16], cols]
            out_ref[4 * g + q] = jnp.concatenate(block, axis=0).astype(bf16)


def columns_kernel(v_ref, core_ref, out_ref):
    second = core_ref[...] > 0.5
    group = lane_index((32, LANES)) // 16
    rows = [jnp.zeros((32, LANES), f32)] * 4
    for s in range(8):
        core, zl = s // 4, s % 4
        cols = [v_ref[core, 4 * zl + q].astype(f32)[16:] for q in range(4)]
        cols = jnp.concatenate(cols, axis=0)
        cols = jnp.where(second, pltpu.roll(cols, N, 1), cols)
        for g in range(4):
            moved = cols if s == g else pltpu.roll(cols, 16 * (s - g) % LANES, 1)
            rows[g] = jnp.where(group == s, moved, rows[g])
    message = jnp.concatenate(rows, axis=0).astype(bf16)
    for i in range(16):
        out_ref[i] = message


def panel_kernel(a_ref, b_ref, out_ref, spread):
    for y in range(4):
        for x in range(4):
            for zl in range(4):
                at = (16 * y + 4 * zl + x) * WIDE
                spread[pl.ds(at, 32), :] = b_ref[4 * y + x, 32 * zl : 32 * zl + 32, :].astype(f32)
    real_lane = lane_index((ROWS, LANES)) % 16 < 8
    upper, lower = [], []
    for q in range(4):
        rows = [a_ref[s // 4, 4 * (s % 4) + q].astype(f32)[:16] for s in range(8)]
        rows = jnp.concatenate(rows, axis=0).T
        turned = jnp.where(real_lane, pltpu.roll(rows, LANES - 8, 1), -pltpu.roll(rows, 8, 1))
        upper.append(rows.astype(bf16))
        lower.append(turned.astype(bf16))
    both = jnp.concatenate(
        [jnp.concatenate(upper, axis=1), jnp.concatenate(lower, axis=1)], axis=0
    )
    for h in range(2):
        columns = []
        for j in range(4 * h, 4 * h + 4):
            parts = [spread[pl.ds(8 * q + j, N, stride=WIDE), :] for q in range(4)]
            columns.append(jnp.concatenate(parts, axis=1))
        part = lax.dot_general(
            both,
            jnp.concatenate(columns, axis=0).astype(bf16),
            (((1,), (1,)), ((), ())),
            preferred_element_type=f32,
        )
        part = part * (1.0 / 16.0)
        out_ref[0, :, h * 256 : (h + 1) * 256] = part[:ROWS]
        out_ref[1, :, h * 256 : (h + 1) * 256] = part[ROWS:]


def call(kernel, shape, dtype, scratch, *args, in_hbm=()):
    vmem = pl.BlockSpec(memory_space=pltpu.VMEM)
    hbm = pl.BlockSpec(memory_space=pltpu.HBM)
    return pl.pallas_call(
        kernel,
        out_shape=jax.ShapeDtypeStruct(shape, dtype),
        in_specs=[hbm if i in in_hbm else vmem for i in range(len(args))],
        out_specs=vmem,
        scratch_shapes=scratch,
        compiler_params=pltpu.CompilerParams(vmem_limit_bytes=32 * 1024 * 1024),
    )(*args)


def shards(
    valence, conduction, band_index, occ_valence, occ_conduction, gap_energy, row_map, col_map
):
    chosen = band_index[0]
    core = lax.axis_index("c")
    mine = chosen // valence.shape[0] == lax.axis_index(COL)
    own = lax.dynamic_index_in_dim(valence, chosen % valence.shape[0], 0, keepdims=False)
    own = jnp.where(mine, own, 0).astype(bf16).reshape(32, LANES)
    both = lax.all_gather(own, "c")
    v = lax.psum(both[0] + both[1], "zh")

    pairs = call(
        pair_kernel,
        (BANDS, N * N + LANES),
        bf16,
        [],
        v,
        conduction.reshape(BANDS, N * N),
        row_map[None],
        col_map[None],
    )
    pairs = pairs.reshape(4, 8, N * N + LANES)
    pairs = lax.all_to_all(pairs, "zl", 0, 0, tiled=True)

    half = call(
        y_kernel,
        (16, ROWS, LANES),
        bf16,
        [pltpu.VMEM((BANDS * WIDE, LANES), f32), pltpu.VMEM((N * WIDE, LANES), f32)],
        pairs.reshape(BANDS, N * N + LANES),
        jnp.asarray(y_table()).astype(bf16),
    )
    block = lax.all_to_all(half, ("y", "x"), 0, 0, tiled=True)

    spots = pairs[:, :4, N * N :]
    spots = jnp.concatenate([spots[:, :2], spots[:, 2:, :COLS]], axis=2)
    hot = (spots[..., None] == jnp.arange(N, dtype=bf16)).astype(bf16)
    table = dot(hot[:, 0], jnp.asarray(x_table()).astype(bf16)).astype(bf16)
    phase = dot(hot[:, 1], jnp.asarray(z_table()).astype(bf16)).astype(bf16)
    weight = 2.0 * (occ_conduction - occ_valence[chosen]).astype(f32) / gap_energy
    weight = lax.dynamic_slice_in_dim(weight, 8 * lax.axis_index("zl"), 8)
    values = call(
        spots_kernel,
        (16, 24, LANES),
        bf16,
        [],
        block,
        table,
        phase,
        jnp.tile(weight, 16)[None],
    )

    values = lax.all_to_all(values, ("zl", "zh"), 0, 0, tiled=True)
    values = lax.all_gather(values, "c")
    cols = call(
        columns_kernel,
        (16, ROWS, LANES),
        bf16,
        [],
        values,
        jnp.full((1, LANES), core, f32),
    )
    columns = lax.all_to_all(cols, ("y", "x"), 0, 0, tiled=True)
    return call(
        panel_kernel,
        (2, ROWS, 8 * N),
        f32,
        [pltpu.VMEM((N * WIDE, LANES), f32)],
        values,
        columns,
    )


def solution(mesh):
    fine = Mesh(mesh.devices.reshape(4, 4, 4, 4, 2), ("y", "zl", "x", "zh", "c"))
    return jax.shard_map(
        shards,
        mesh=fine,
        in_specs=(
            P(COL, GA, None),
            P(COL, GA, None),
            P(),
            P(),
            P(COL),
            P(COL),
            P(GA),
            P(GA),
        ),
        out_specs=P(None, GA, COL),
        check_vma=False,
    )
```

```python
import jax
import jax.numpy as jnp
import numpy as np
from jax import lax
from jax.experimental import pallas as pl
from jax.experimental.pallas import tpu as pltpu
from jax.sharding import Mesh
from jax.sharding import PartitionSpec as P

N = 64
BANDS = 32
ROWS = 128
COLS = 64
SPOTS = ROWS + COLS
LANES = 128
WIDE = 40
GA = ("y", "zl", "x")
COL = ("zh", "c")

f32 = jnp.float32
bf16 = jnp.bfloat16


def dot(left, right):
    return jnp.dot(left, right, preferred_element_type=f32)


def lane_index(shape):
    return lax.broadcasted_iota(jnp.int32, shape, len(shape) - 1)


def y_table():
    parity = np.arange(2)[:, None, None, None]
    imag = np.arange(2)[None, :, None, None]
    ky = np.arange(N // 2)[None, None, :, None]
    half = np.arange(N // 2)[None, None, None, :]
    turn = (ky * (2 * half + parity) + 16 * imag) % N
    return wave(turn).reshape(LANES, N // 2)


def wave(turn):
    return (np.cos(2.0 * np.pi * (turn % N) / N) / 8.0).astype(np.float32)


def x_table():
    kx = np.arange(N)[:, None]
    lane = np.arange(LANES)[None, :]
    plane, imag = lane // 8, lane // 4 % 2
    x = 16 * (plane // 4) + 4 * (lane % 4) + plane % 4
    return np.concatenate([wave(kx * x - 16 * imag), wave(kx * x + 16 * (1 - imag))], axis=1)


def z_table():
    turn = np.arange(N)[:, None] * (np.arange(LANES)[None, :] % N)
    return np.concatenate([wave(turn), wave(turn - 16)], axis=1)


def pair_kernel(v_ref, c_ref, row_ref, col_ref, out_ref):
    v = v_ref[...].astype(f32)
    for i in range(N // 2):
        lanes = pl.ds(i * LANES, LANES)
        out_ref[:, lanes] = (c_ref[:, lanes].astype(f32) * v[i : i + 1, :]).astype(bf16)
    row = row_ref[...]
    col = jnp.concatenate([col_ref[...]] * 2, axis=1)
    spots = [row >> 6, row & (N - 1), col >> 6, col & (N - 1)]
    spots = jnp.concatenate(spots * 2, axis=0).astype(f32)
    out_ref[:, N * N :] = jnp.concatenate([spots] * 4, axis=0).astype(bf16)


def y_kernel(p_ref, e_ref, out_ref, by_row, by_ky):
    for i in range(N // 2):
        by_row[pl.ds(i, BANDS, stride=WIDE), :] = p_ref[:, i * LANES : (i + 1) * LANES].astype(f32)
    table = e_ref[...]
    low = lane_index((N, LANES)) < N
    half = N // 2
    for j in range(BANDS // 2):
        first = by_row[pl.ds(2 * WIDE * j, half), :]
        second = by_row[pl.ds(2 * WIDE * j + WIDE, half), :]
        both = dot(table, jnp.concatenate([first, second], axis=1).astype(bf16))
        even, odd = both[:N], both[N:]
        even = jnp.where(low, even[:, :LANES], pltpu.roll(even[:, LANES:], N, 1))
        odd = jnp.where(low, pltpu.roll(odd[:, :LANES], N, 1), odd[:, LANES:])
        at = 8 * (j % 4) + j // 4
        for start, value in ((at, even + odd), (half * WIDE + at, even - odd)):
            by_ky[pl.ds(start, half, stride=WIDE), :] = value[:half]
            by_ky[pl.ds(start + 4, half, stride=WIDE), :] = value[half:]
    for ky in range(N):
        y, zl, x = ky // 16, ky // 4 % 4, ky % 4
        out_ref[4 * y + x, 32 * zl : 32 * zl + 32, :] = by_ky[pl.ds(ky * WIDE, 32), :].astype(bf16)


def spots_kernel(r_ref, e_ref, p_ref, w_ref, out_ref):
    column = lane_index((2 * LANES, LANES))
    band = lax.broadcasted_iota(jnp.int32, (2 * LANES, LANES), 0) // N
    total = jnp.zeros((2 * SPOTS, LANES), f32)
    for g in range(4):
        planes = r_ref[:, 32 * g : 32 * g + 32, :].astype(f32)
        table = jnp.concatenate([e_ref[g, :, :LANES], e_ref[g, :, LANES:]], axis=0)
        cos_z = jnp.concatenate([p_ref[g, :, :LANES].astype(f32)] * 2, axis=1)
        sin_z = jnp.concatenate([p_ref[g, :, LANES:].astype(f32)] * 2, axis=1)
        for h in range(2):
            first = planes[:, 16 * h : 16 * h + 8, :].reshape(LANES, LANES)
            second = planes[:, 16 * h + 8 : 16 * h + 16, :].reshape(LANES, LANES)
            at_x = dot(table, jnp.concatenate([first, second], axis=1).astype(bf16))
            real, imag = at_x[:SPOTS], at_x[SPOTS:]
            real_z = real * cos_z + imag * sin_z
            imag_z = imag * cos_z - real * sin_z
            terms = jnp.concatenate([real_z, imag_z], axis=0).astype(bf16)
            ones = jnp.where(column == band + 16 * g + 4 * h, 1.0, 0.0).astype(bf16)
            total = total + dot(terms, ones)
    joined = total[:SPOTS] + pltpu.roll(total[SPOTS:], 8, 1)
    rows = (joined[:ROWS] * w_ref[0:1, :]).T
    for q in range(4):
        cols = joined[ROWS + 16 * q : ROWS + 16 * q + 16]
        cols = cols[:8] + pltpu.roll(cols[8:], N, 1)
        for g in range(4):
            block = [rows[16 * g : 16 * g + 16], cols]
            out_ref[4 * g + q] = jnp.concatenate(block, axis=0).astype(bf16)


def columns_kernel(v_ref, core_ref, out_ref):
    second = core_ref[1:2, :] > 0.5
    group = lane_index((32, LANES)) // 16
    rows = [jnp.zeros((32, LANES), f32)] * 4
    for s in range(8):
        core, zl = s // 4, s % 4
        cols = [v_ref[core, 4 * zl + q].astype(f32)[16:] for q in range(4)]
        cols = jnp.concatenate(cols, axis=0)
        cols = jnp.where(second, pltpu.roll(cols, N, 1), cols)
        for g in range(4):
            moved = cols if s == g else pltpu.roll(cols, 16 * (s - g) % LANES, 1)
            rows[g] = jnp.where(group == s, moved, rows[g])
    message = jnp.concatenate(rows, axis=0).astype(bf16)
    for i in range(16):
        out_ref[i] = message


def panel_kernel(a_ref, b_ref, out_ref, spread):
    for y in range(4):
        for x in range(4):
            for zl in range(4):
                at = (16 * y + 4 * zl + x) * WIDE
                spread[pl.ds(at, 32), :] = b_ref[4 * y + x, 32 * zl : 32 * zl + 32, :].astype(f32)
    real_lane = lane_index((ROWS, LANES)) % 16 < 8
    upper, lower = [], []
    for q in range(4):
        rows = [a_ref[s // 4, 4 * (s % 4) + q].astype(f32)[:16] for s in range(8)]
        rows = jnp.concatenate(rows, axis=0).T
        turned = jnp.where(real_lane, pltpu.roll(rows, LANES - 8, 1), -pltpu.roll(rows, 8, 1))
        upper.append(rows.astype(bf16))
        lower.append(turned.astype(bf16))
    both = jnp.concatenate(
        [jnp.concatenate(upper, axis=1), jnp.concatenate(lower, axis=1)], axis=0
    )
    for h in range(2):
        columns = []
        for j in range(4 * h, 4 * h + 4):
            parts = [spread[pl.ds(8 * q + j, N, stride=WIDE), :] for q in range(4)]
            columns.append(jnp.concatenate(parts, axis=1))
        part = lax.dot_general(
            both,
            jnp.concatenate(columns, axis=0).astype(bf16),
            (((1,), (1,)), ((), ())),
            preferred_element_type=f32,
        )
        part = part * (1.0 / 16.0)
        out_ref[0, :, h * 256 : (h + 1) * 256] = part[:ROWS]
        out_ref[1, :, h * 256 : (h + 1) * 256] = part[ROWS:]


def call(kernel, shape, dtype, scratch, *args):
    vmem = pl.BlockSpec(memory_space=pltpu.VMEM)
    return pl.pallas_call(
        kernel,
        out_shape=jax.ShapeDtypeStruct(shape, dtype),
        in_specs=[vmem] * len(args),
        out_specs=vmem,
        scratch_shapes=scratch,
        compiler_params=pltpu.CompilerParams(vmem_limit_bytes=32 * 1024 * 1024),
    )(*args)


def shards(
    valence, conduction, band_index, occ_valence, occ_conduction, gap_energy, row_map, col_map
):
    chosen = band_index[0]
    core = lax.axis_index("c")
    mine = chosen // valence.shape[0] == lax.axis_index(COL)
    own = lax.dynamic_index_in_dim(valence, chosen % valence.shape[0], 0, keepdims=False)
    own = jnp.where(mine, own, 0).astype(bf16).reshape(32, LANES)
    both = lax.all_gather(own, "c")
    v = lax.psum(both[0] + both[1], "zh")

    pairs = call(
        pair_kernel,
        (BANDS, N * N + LANES),
        bf16,
        [],
        v,
        conduction.reshape(BANDS, N * N),
        row_map[None],
        col_map[None],
    )
    pairs = pairs.reshape(4, 8, N * N + LANES)
    pairs = lax.all_to_all(pairs, "zl", 0, 0, tiled=True)
    late = lax.optimization_barrier((pairs, occ_valence, occ_conduction, gap_energy))
    pairs, occ_valence, occ_conduction, gap_energy = late

    half = call(
        y_kernel,
        (16, ROWS, LANES),
        bf16,
        [pltpu.VMEM((BANDS * WIDE, LANES), f32), pltpu.VMEM((N * WIDE, LANES), f32)],
        pairs.reshape(BANDS, N * N + LANES),
        jnp.asarray(y_table()).astype(bf16),
    )
    block = lax.all_to_all(half, ("y", "x"), 0, 0, tiled=True)

    spots = pairs[:, :4, N * N :]
    spots = jnp.concatenate([spots[:, :2], spots[:, 2:, :COLS]], axis=2)
    hot = (spots[..., None] == jnp.arange(N, dtype=bf16)).astype(bf16)
    table = dot(hot[:, 0], jnp.asarray(x_table()).astype(bf16)).astype(bf16)
    phase = dot(hot[:, 1], jnp.asarray(z_table()).astype(bf16)).astype(bf16)
    weight = 2.0 * (occ_conduction - occ_valence[chosen]).astype(f32) / gap_energy
    weight = lax.dynamic_slice_in_dim(weight, 8 * lax.axis_index("zl"), 8)
    scales = jnp.stack([jnp.tile(weight, 16), jnp.full((LANES,), core, f32)])
    values = call(
        spots_kernel,
        (16, 24, LANES),
        bf16,
        [],
        block,
        table,
        phase,
        scales,
    )

    values = lax.all_to_all(values, ("zl", "zh"), 0, 0, tiled=True)
    values = lax.all_gather(values, "c")
    cols = call(
        columns_kernel,
        (16, ROWS, LANES),
        bf16,
        [],
        values,
        scales,
    )
    columns = lax.all_to_all(cols, ("y", "x"), 0, 0, tiled=True)
    return call(
        panel_kernel,
        (2, ROWS, 8 * N),
        f32,
        [pltpu.VMEM((N * WIDE, LANES), f32)],
        values,
        columns,
    )


def solution(mesh):
    fine = Mesh(mesh.devices.reshape(4, 4, 4, 4, 2), ("y", "zl", "x", "zh", "c"))
    return jax.shard_map(
        shards,
        mesh=fine,
        in_specs=(
            P(COL, GA, None),
            P(COL, GA, None),
            P(),
            P(),
            P(COL),
            P(COL),
            P(GA),
            P(GA),
        ),
        out_specs=P(None, GA, COL),
        check_vma=False,
    )
```

```python
import jax
import jax.numpy as jnp
import numpy as np
from jax import lax
from jax.experimental import pallas as pl
from jax.experimental.pallas import tpu as pltpu
from jax.sharding import Mesh
from jax.sharding import PartitionSpec as P

N = 64
BANDS = 32
ROWS = 128
COLS = 64
SPOTS = ROWS + COLS
LANES = 128
WIDE = 40
GA = ("y", "zl", "x")
COL = ("zh", "c")

f32 = jnp.float32
bf16 = jnp.bfloat16


def dot(left, right):
    return jnp.dot(left, right, preferred_element_type=f32)


def lane_index(shape):
    return lax.broadcasted_iota(jnp.int32, shape, len(shape) - 1)


def y_table():
    parity = np.arange(2)[:, None, None, None]
    imag = np.arange(2)[None, :, None, None]
    ky = np.arange(N // 2)[None, None, :, None]
    half = np.arange(N // 2)[None, None, None, :]
    turn = (ky * (2 * half + parity) + 16 * imag) % N
    return wave(turn).reshape(LANES, N // 2)


def wave(turn):
    return (np.cos(2.0 * np.pi * (turn % N) / N) / 8.0).astype(np.float32)


def x_table():
    kx = np.arange(N)[:, None]
    lane = np.arange(LANES)[None, :]
    plane, imag = lane // 8, lane // 4 % 2
    x = 16 * (plane // 4) + 4 * (lane % 4) + plane % 4
    return np.concatenate([wave(kx * x - 16 * imag), wave(kx * x + 16 * (1 - imag))], axis=1)


def z_table():
    turn = np.arange(N)[:, None] * (np.arange(LANES)[None, :] % N)
    return np.concatenate([wave(turn), wave(turn - 16)], axis=1)


def pair_kernel(v_ref, c_ref, row_ref, col_ref, e_ref, out_ref):
    v = v_ref[...].astype(f32)
    for i in range(N // 2):
        lanes = pl.ds(i * LANES, LANES)
        out_ref[:, lanes] = (c_ref[:, lanes].astype(f32) * v[i : i + 1, :]).astype(bf16)
    row = row_ref[...]
    col = jnp.concatenate([col_ref[...]] * 2, axis=1)
    spots = [row >> 6, row & (N - 1), col >> 6, col & (N - 1)]
    spots = jnp.concatenate(spots * 2, axis=0).astype(f32)
    out_ref[:, N * N :] = jnp.concatenate([spots] * 4, axis=0).astype(bf16)


def y_kernel(p_ref, e_ref, out_ref, by_row, by_ky):
    for i in range(N // 2):
        by_row[pl.ds(i, BANDS, stride=WIDE), :] = p_ref[:, i * LANES : (i + 1) * LANES].astype(f32)
    table = e_ref[...]
    low = lane_index((N, LANES)) < N
    half = N // 2
    for j in range(BANDS // 2):
        first = by_row[pl.ds(2 * WIDE * j, half), :]
        second = by_row[pl.ds(2 * WIDE * j + WIDE, half), :]
        both = dot(table, jnp.concatenate([first, second], axis=1).astype(bf16))
        even, odd = both[:N], both[N:]
        even = jnp.where(low, even[:, :LANES], pltpu.roll(even[:, LANES:], N, 1))
        odd = jnp.where(low, pltpu.roll(odd[:, :LANES], N, 1), odd[:, LANES:])
        at = 8 * (j % 4) + j // 4
        for start, value in ((at, even + odd), (half * WIDE + at, even - odd)):
            by_ky[pl.ds(start, half, stride=WIDE), :] = value[:half]
            by_ky[pl.ds(start + 4, half, stride=WIDE), :] = value[half:]
    for ky in range(N):
        y, zl, x = ky // 16, ky // 4 % 4, ky % 4
        out_ref[4 * y + x, 32 * zl : 32 * zl + 32, :] = by_ky[pl.ds(ky * WIDE, 32), :].astype(bf16)


def spots_kernel(r_ref, e_ref, p_ref, w_ref, out_ref):
    column = lane_index((2 * LANES, LANES))
    band = lax.broadcasted_iota(jnp.int32, (2 * LANES, LANES), 0) // N
    total = jnp.zeros((2 * SPOTS, LANES), f32)
    for g in range(4):
        planes = r_ref[:, 32 * g : 32 * g + 32, :].astype(f32)
        table = jnp.concatenate([e_ref[g, :, :LANES], e_ref[g, :, LANES:]], axis=0)
        cos_z = jnp.concatenate([p_ref[g, :, :LANES].astype(f32)] * 2, axis=1)
        sin_z = jnp.concatenate([p_ref[g, :, LANES:].astype(f32)] * 2, axis=1)
        for h in range(2):
            first = planes[:, 16 * h : 16 * h + 8, :].reshape(LANES, LANES)
            second = planes[:, 16 * h + 8 : 16 * h + 16, :].reshape(LANES, LANES)
            at_x = dot(table, jnp.concatenate([first, second], axis=1).astype(bf16))
            real, imag = at_x[:SPOTS], at_x[SPOTS:]
            real_z = real * cos_z + imag * sin_z
            imag_z = imag * cos_z - real * sin_z
            terms = jnp.concatenate([real_z, imag_z], axis=0).astype(bf16)
            ones = jnp.where(column == band + 16 * g + 4 * h, 1.0, 0.0).astype(bf16)
            total = total + dot(terms, ones)
    joined = total[:SPOTS] + pltpu.roll(total[SPOTS:], 8, 1)
    rows = (joined[:ROWS] * w_ref[0:1, :]).T
    for q in range(4):
        cols = joined[ROWS + 16 * q : ROWS + 16 * q + 16]
        cols = cols[:8] + pltpu.roll(cols[8:], N, 1)
        for g in range(4):
            block = [rows[16 * g : 16 * g + 16], cols]
            out_ref[4 * q + g] = jnp.concatenate(block, axis=0).astype(bf16)


def columns_kernel(v_ref, core_ref, out_ref):
    second = core_ref[1:2, :] > 0.5
    group = lane_index((32, LANES)) // 16
    rows = [jnp.zeros((32, LANES), f32)] * 4
    for s in range(8):
        core, zl = s // 4, s % 4
        cols = [v_ref[core, 4 * q + zl].astype(f32)[16:] for q in range(4)]
        cols = jnp.concatenate(cols, axis=0)
        cols = jnp.where(second, pltpu.roll(cols, N, 1), cols)
        for g in range(4):
            moved = cols if s == g else pltpu.roll(cols, 16 * (s - g) % LANES, 1)
            rows[g] = jnp.where(group == s, moved, rows[g])
    message = jnp.concatenate(rows, axis=0).astype(bf16)
    for i in range(16):
        out_ref[i] = message


def panel_kernel(a_ref, b_ref, out_ref, spread):
    for y in range(4):
        for x in range(4):
            for zl in range(4):
                at = (16 * y + 4 * zl + x) * WIDE
                spread[pl.ds(at, 32), :] = b_ref[4 * y + x, 32 * zl : 32 * zl + 32, :].astype(f32)
    real_lane = lane_index((ROWS, LANES)) % 16 < 8
    upper, lower = [], []
    for q in range(4):
        rows = [a_ref[s // 4, 4 * q + s % 4].astype(f32)[:16] for s in range(8)]
        rows = jnp.concatenate(rows, axis=0).T
        turned = jnp.where(real_lane, pltpu.roll(rows, LANES - 8, 1), -pltpu.roll(rows, 8, 1))
        upper.append(rows.astype(bf16))
        lower.append(turned.astype(bf16))
    both = jnp.concatenate(
        [jnp.concatenate(upper, axis=1), jnp.concatenate(lower, axis=1)], axis=0
    )
    for h in range(2):
        columns = []
        for j in range(4 * h, 4 * h + 4):
            parts = [spread[pl.ds(8 * q + j, N, stride=WIDE), :] for q in range(4)]
            columns.append(jnp.concatenate(parts, axis=1))
        part = lax.dot_general(
            both,
            jnp.concatenate(columns, axis=0).astype(bf16),
            (((1,), (1,)), ((), ())),
            preferred_element_type=f32,
        )
        part = part * (1.0 / 16.0)
        out_ref[0, :, h * 256 : (h + 1) * 256] = part[:ROWS]
        out_ref[1, :, h * 256 : (h + 1) * 256] = part[ROWS:]


def call(kernel, shape, dtype, scratch, *args):
    vmem = pl.BlockSpec(memory_space=pltpu.VMEM)
    return pl.pallas_call(
        kernel,
        out_shape=jax.ShapeDtypeStruct(shape, dtype),
        in_specs=[vmem] * len(args),
        out_specs=vmem,
        scratch_shapes=scratch,
        compiler_params=pltpu.CompilerParams(vmem_limit_bytes=32 * 1024 * 1024),
    )(*args)


def shards(
    valence, conduction, band_index, occ_valence, occ_conduction, gap_energy, row_map, col_map
):
    chosen = band_index[0]
    core = lax.axis_index("c")
    local = lax.all_gather(valence.reshape(-1, N * N), "c", tiled=True)
    own = lax.dynamic_index_in_dim(local, chosen % local.shape[0], 0, keepdims=False)
    own = jnp.where(chosen // local.shape[0] == lax.axis_index("zh"), own, 0)
    v = lax.psum(own.astype(bf16).reshape(32, LANES), "zh")

    table_y = jnp.asarray(y_table()).astype(bf16)
    pairs = call(
        pair_kernel,
        (BANDS, N * N + LANES),
        bf16,
        [],
        v,
        conduction.reshape(BANDS, N * N),
        row_map[None],
        col_map[None],
        table_y,
    )
    pairs = pairs.reshape(4, 8, N * N + LANES)
    pairs = lax.all_to_all(pairs, "zl", 0, 0, tiled=True)
    late = lax.optimization_barrier((pairs, occ_valence, occ_conduction, gap_energy))
    pairs, occ_valence, occ_conduction, gap_energy = late

    half = call(
        y_kernel,
        (16, ROWS, LANES),
        bf16,
        [pltpu.VMEM((BANDS * WIDE, LANES), f32), pltpu.VMEM((N * WIDE, LANES), f32)],
        pairs.reshape(BANDS, N * N + LANES),
        table_y,
    )
    block = lax.all_to_all(half, ("y", "x"), 0, 0, tiled=True)

    spots = pairs[:, :4, N * N :]
    spots = jnp.concatenate([spots[:, :2], spots[:, 2:, :COLS]], axis=2)
    hot = (spots[..., None] == jnp.arange(N, dtype=bf16)).astype(bf16)
    table = dot(hot[:, 0], jnp.asarray(x_table()).astype(bf16)).astype(bf16)
    phase = dot(hot[:, 1], jnp.asarray(z_table()).astype(bf16)).astype(bf16)
    weight = 2.0 * (occ_conduction - occ_valence[chosen]).astype(f32) / gap_energy
    weight = lax.dynamic_slice_in_dim(weight, 8 * lax.axis_index("zl"), 8)
    scales = jnp.stack([jnp.tile(weight, 16), jnp.full((LANES,), core, f32)])
    values = call(
        spots_kernel,
        (16, 24, LANES),
        bf16,
        [],
        block,
        table,
        phase,
        scales,
    )

    values = lax.all_to_all(values, ("zh", "zl"), 0, 0, tiled=True)
    values = lax.all_gather(values, "c")
    cols = call(
        columns_kernel,
        (16, ROWS, LANES),
        bf16,
        [],
        values,
        scales,
    )
    columns = lax.all_to_all(cols, ("y", "x"), 0, 0, tiled=True)
    return call(
        panel_kernel,
        (2, ROWS, 8 * N),
        f32,
        [pltpu.VMEM((N * WIDE, LANES), f32)],
        values,
        columns,
    )


def solution(mesh):
    fine = Mesh(mesh.devices.reshape(4, 4, 4, 4, 2), ("y", "zl", "x", "zh", "c"))
    return jax.shard_map(
        shards,
        mesh=fine,
        in_specs=(
            P(COL, GA, None),
            P(COL, GA, None),
            P(),
            P(),
            P(COL),
            P(COL),
            P(GA),
            P(GA),
        ),
        out_specs=P(None, GA, COL),
        check_vma=False,
    )
```

```python
import jax
import jax.numpy as jnp
import numpy as np
from jax import lax
from jax.experimental import pallas as pl
from jax.experimental.pallas import tpu as pltpu
from jax.sharding import Mesh
from jax.sharding import PartitionSpec as P

N = 64
BANDS = 32
ROWS = 128
COLS = 64
SPOTS = ROWS + COLS
LANES = 128
WIDE = 40
GA = ("y", "zl", "x")
COL = ("zh", "c")

f32 = jnp.float32
bf16 = jnp.bfloat16


def dot(left, right):
    return jnp.dot(left, right, preferred_element_type=f32)


def lane_index(shape):
    return lax.broadcasted_iota(jnp.int32, shape, len(shape) - 1)


def y_table():
    parity = np.arange(2)[:, None, None, None]
    imag = np.arange(2)[None, :, None, None]
    ky = np.arange(N // 2)[None, None, :, None]
    half = np.arange(N // 2)[None, None, None, :]
    turn = (ky * (2 * half + parity) + 16 * imag) % N
    return wave(turn).reshape(LANES, N // 2)


def wave(turn):
    return (np.cos(2.0 * np.pi * (turn % N) / N) / 8.0).astype(np.float32)


def x_table():
    kx = np.arange(N)[:, None]
    x, imag = np.arange(LANES)[None, :] % N, np.arange(LANES)[None, :] // N
    return np.concatenate([wave(kx * x - 16 * imag), wave(kx * x + 16 * (1 - imag))], axis=1)


def z_table():
    turn = np.arange(N)[:, None] * (np.arange(LANES)[None, :] % N)
    return np.concatenate([wave(turn), wave(turn - 16)], axis=1)


def pair_y_kernel(v_ref, c_ref, e_ref, out_ref, by_row, by_ky):
    v = v_ref[...].astype(f32)
    for i in range(N // 2):
        bands = c_ref[:, i * LANES : (i + 1) * LANES].astype(f32)
        pair = (bands * v[i : i + 1, :]).astype(bf16).astype(f32)
        by_row[pl.ds(i, BANDS, stride=WIDE), :] = pair
    table = e_ref[...]
    low = lane_index((N, LANES)) < N
    half = N // 2
    for j in range(BANDS // 2):
        first = by_row[pl.ds(2 * WIDE * j, half), :]
        second = by_row[pl.ds(2 * WIDE * j + WIDE, half), :]
        both = dot(table, jnp.concatenate([first, second], axis=1).astype(bf16))
        even, odd = both[:N], both[N:]
        even = jnp.where(low, even[:, :LANES], pltpu.roll(even[:, LANES:], N, 1))
        odd = jnp.where(low, pltpu.roll(odd[:, :LANES], N, 1), odd[:, LANES:])
        for start, value in ((2 * j, even + odd), (half * WIDE + 2 * j, even - odd)):
            by_ky[pl.ds(start, half, stride=WIDE), :] = value[:half]
            by_ky[pl.ds(start + 1, half, stride=WIDE), :] = value[half:]
    for place in range(N):
        first, zl = place // 16 * 16 + place % 4, place // 4 % 4
        rows = [by_ky[pl.ds((first + 4 * k) * WIDE + 8 * zl, 8), :] for k in range(4)]
        out_ref[place] = jnp.concatenate(rows, axis=0).astype(bf16)


def weight_row(place_ref, occ_v_ref, occ_c_ref, gap_ref):
    lane = lane_index((1, LANES))
    chosen = jnp.where(lane == place_ref[0:1, :], occ_v_ref[...], 0).astype(f32)
    filled = jnp.sum(chosen, axis=1, keepdims=True)
    weight = 2.0 * (occ_c_ref[...].astype(f32) - filled) / gap_ref[...]
    band = lax.broadcasted_iota(jnp.int32, (BANDS, LANES), 0)
    pick = jnp.where(band == place_ref[1:2, :] + lane % 8, 1.0, 0.0)
    return jnp.dot(weight, pick, precision=lax.Precision.HIGHEST, preferred_element_type=f32)


def spots_kernel(
    r_ref, e_ref, p_ref, place_ref, occ_v_ref, occ_c_ref, gap_ref, out_ref, planes
):
    for x in range(N):
        planes[pl.ds(x * WIDE, 32), :] = r_ref[x].astype(f32)
    column = lane_index((2 * LANES, LANES))
    band = lax.broadcasted_iota(jnp.int32, (2 * LANES, LANES), 0) // N
    total = jnp.zeros((2 * SPOTS, LANES), f32)
    for g in range(4):
        table = jnp.concatenate([e_ref[g, :, :LANES], e_ref[g, :, LANES:]], axis=0)
        cos_z = jnp.concatenate([p_ref[g, :, :LANES].astype(f32)] * 2, axis=1)
        sin_z = jnp.concatenate([p_ref[g, :, LANES:].astype(f32)] * 2, axis=1)
        for h in range(2):
            both = []
            for row in (8 * g + 4 * h, 8 * g + 4 * h + 2):
                parts = [planes[pl.ds(row + k, N, stride=WIDE), :] for k in range(2)]
                both.append(jnp.concatenate(parts, axis=0))
            first, second = both
            at_x = dot(table, jnp.concatenate([first, second], axis=1).astype(bf16))
            real, imag = at_x[:SPOTS], at_x[SPOTS:]
            real_z = real * cos_z + imag * sin_z
            imag_z = imag * cos_z - real * sin_z
            terms = jnp.concatenate([real_z, imag_z], axis=0).astype(bf16)
            ones = jnp.where(column == band + 16 * g + 4 * h, 1.0, 0.0).astype(bf16)
            total = total + dot(terms, ones)
    joined = total[:SPOTS] + pltpu.roll(total[SPOTS:], 8, 1)
    rows = (joined[:ROWS] * weight_row(place_ref, occ_v_ref, occ_c_ref, gap_ref)).T
    for q in range(4):
        cols = joined[ROWS + 16 * q : ROWS + 16 * q + 16]
        cols = cols[:8] + pltpu.roll(cols[8:], N, 1)
        for g in range(4):
            block = [rows[16 * g : 16 * g + 16], cols, jnp.zeros_like(cols)]
            out_ref[4 * q + g] = jnp.concatenate(block, axis=0).astype(bf16)


def columns_kernel(v_ref, core_ref, out_ref):
    second = core_ref[2:3, :] > 0
    group = lane_index((32, LANES)) // 16
    rows = [jnp.zeros((32, LANES), f32)] * 4
    for s in range(8):
        core, zl = s // 4, s % 4
        cols = [v_ref[core, 4 * q + zl, 16:].astype(f32)[:8] for q in range(4)]
        cols = jnp.concatenate(cols, axis=0)
        cols = jnp.where(second, pltpu.roll(cols, N, 1), cols)
        for g in range(4):
            moved = cols if s == g else pltpu.roll(cols, 16 * (s - g) % LANES, 1)
            rows[g] = jnp.where(group == s, moved, rows[g])
    message = jnp.concatenate(rows, axis=0).astype(bf16)
    for i in range(16):
        out_ref[i] = message


def panel_kernel(a_ref, b_ref, out_ref, spread):
    for y in range(4):
        for x in range(4):
            for zl in range(4):
                at = (16 * y + 4 * zl + x) * WIDE
                spread[pl.ds(at, 32), :] = b_ref[4 * y + x, 32 * zl : 32 * zl + 32, :].astype(f32)
    real_lane = lane_index((ROWS, LANES)) % 16 < 8
    upper, lower = [], []
    for q in range(4):
        rows = [a_ref[s // 4, 4 * q + s % 4, :16].astype(f32) for s in range(8)]
        rows = jnp.concatenate(rows, axis=0).T
        turned = jnp.where(real_lane, pltpu.roll(rows, LANES - 8, 1), -pltpu.roll(rows, 8, 1))
        upper.append(rows.astype(bf16))
        lower.append(turned.astype(bf16))
    both = jnp.concatenate(
        [jnp.concatenate(upper, axis=1), jnp.concatenate(lower, axis=1)], axis=0
    )
    for h in range(2):
        columns = []
        for j in range(4 * h, 4 * h + 4):
            parts = [spread[pl.ds(8 * q + j, N, stride=WIDE), :] for q in range(4)]
            columns.append(jnp.concatenate(parts, axis=1))
        part = lax.dot_general(
            both,
            jnp.concatenate(columns, axis=0).astype(bf16),
            (((1,), (1,)), ((), ())),
            preferred_element_type=f32,
        )
        part = part * (1.0 / 16.0)
        out_ref[0, :, h * 256 : (h + 1) * 256] = part[:ROWS]
        out_ref[1, :, h * 256 : (h + 1) * 256] = part[ROWS:]


def call(kernel, shape, dtype, scratch, *args):
    vmem = pl.BlockSpec(memory_space=pltpu.VMEM)
    return pl.pallas_call(
        kernel,
        out_shape=jax.ShapeDtypeStruct(shape, dtype),
        in_specs=[vmem] * len(args),
        out_specs=vmem,
        scratch_shapes=scratch,
        compiler_params=pltpu.CompilerParams(vmem_limit_bytes=32 * 1024 * 1024),
    )(*args)


def shards(
    valence, conduction, band_index, occ_valence, occ_conduction, gap_energy, row_map, col_map
):
    chosen = band_index[0]
    core = lax.axis_index("c")
    local = lax.all_gather(valence.reshape(-1, N * N), "c", tiled=True)
    own = lax.dynamic_index_in_dim(local, chosen % local.shape[0], 0, keepdims=False)
    own = jnp.where(chosen // local.shape[0] == lax.axis_index("zh"), own, 0)
    v = lax.psum(own.astype(bf16).reshape(32, LANES), "zh")

    half = call(
        pair_y_kernel,
        (N, 32, LANES),
        bf16,
        [pltpu.VMEM((BANDS * WIDE, LANES), f32), pltpu.VMEM((N * WIDE, LANES), f32)],
        v,
        conduction.reshape(BANDS, N * N),
        jnp.asarray(y_table()).astype(bf16),
    )
    half, row_map, col_map = lax.optimization_barrier((half, row_map, col_map))
    block = lax.all_to_all(half, GA, 0, 0, tiled=True)

    spots = jnp.concatenate([row_map, col_map])
    spots = lax.all_gather(spots, "zl")
    grid = jnp.arange(N, dtype=jnp.int32)
    table = dot(((spots >> 6)[..., None] == grid).astype(bf16), jnp.asarray(x_table()).astype(bf16))
    phase = dot(((spots & 63)[..., None] == grid).astype(bf16), jnp.asarray(z_table()).astype(bf16))
    places = jnp.stack([chosen, 8 * lax.axis_index("zl"), core])
    places = jnp.broadcast_to(places[:, None], (3, LANES))
    values = call(
        spots_kernel,
        (16, 32, LANES),
        bf16,
        [pltpu.VMEM((N * WIDE, LANES), f32)],
        block,
        table.astype(bf16),
        phase.astype(bf16),
        places,
        occ_valence[None],
        occ_conduction[None],
        gap_energy[None],
    )

    values = lax.all_to_all(values, ("zh", "zl"), 0, 0, tiled=True)
    values = lax.all_gather(values, "c")
    cols = call(
        columns_kernel,
        (16, ROWS, LANES),
        bf16,
        [],
        values,
        places,
    )
    columns = lax.all_to_all(cols, ("y", "x"), 0, 0, tiled=True)
    return call(
        panel_kernel,
        (2, ROWS, 8 * N),
        f32,
        [pltpu.VMEM((N * WIDE, LANES), f32)],
        values,
        columns,
    )


def solution(mesh):
    fine = Mesh(mesh.devices.reshape(4, 4, 4, 4, 2), ("y", "zl", "x", "zh", "c"))
    return jax.shard_map(
        shards,
        mesh=fine,
        in_specs=(
            P(COL, GA, None),
            P(COL, GA, None),
            P(),
            P(),
            P(COL),
            P(COL),
            P(GA),
            P(GA),
        ),
        out_specs=P(None, GA, COL),
        check_vma=False,
    )
```

```python
import jax
import jax.numpy as jnp
import numpy as np
from jax import lax
from jax.experimental import pallas as pl
from jax.experimental.pallas import tpu as pltpu
from jax.sharding import Mesh
from jax.sharding import PartitionSpec as P

N = 64
BANDS = 32
ROWS = 128
COLS = 64
SPOTS = ROWS + COLS
LANES = 128
WIDE = 40
GA = ("y", "zl", "x")
COL = ("zh", "c")

f32 = jnp.float32
bf16 = jnp.bfloat16


def dot(left, right):
    return jnp.dot(left, right, preferred_element_type=f32)


def lane_index(shape):
    return lax.broadcasted_iota(jnp.int32, shape, len(shape) - 1)


def y_table():
    parity = np.arange(2)[:, None, None, None]
    imag = np.arange(2)[None, :, None, None]
    ky = np.arange(N // 2)[None, None, :, None]
    half = np.arange(N // 2)[None, None, None, :]
    turn = (ky * (2 * half + parity) + 16 * imag) % N
    return wave(turn).reshape(LANES, N // 2)


def wave(turn):
    return (np.cos(2.0 * np.pi * (turn % N) / N) / 8.0).astype(np.float32)


def x_table():
    kx = np.arange(N)[:, None]
    x, imag = np.arange(LANES)[None, :] % N, np.arange(LANES)[None, :] // N
    return np.concatenate([wave(kx * x - 16 * imag), wave(kx * x + 16 * (1 - imag))], axis=1)


def z_table():
    turn = np.arange(N)[:, None] * (np.arange(LANES)[None, :] % N)
    return np.concatenate([wave(turn), wave(turn - 16)], axis=1)


def pair_y_kernel(v_ref, c_ref, e_ref, out_ref, by_row, by_ky):
    v = v_ref[...].astype(f32)
    for i in range(N // 2):
        bands = c_ref[:, i * LANES : (i + 1) * LANES].astype(f32)
        pair = (bands * v[i : i + 1, :]).astype(bf16).astype(f32)
        by_row[pl.ds(i, BANDS, stride=WIDE), :] = pair
    table = e_ref[...]
    low = lane_index((N, LANES)) < N
    half = N // 2
    for j in range(BANDS // 2):
        first = by_row[pl.ds(2 * WIDE * j, half), :]
        second = by_row[pl.ds(2 * WIDE * j + WIDE, half), :]
        both = dot(table, jnp.concatenate([first, second], axis=1).astype(bf16))
        even, odd = both[:N], both[N:]
        even = jnp.where(low, even[:, :LANES], pltpu.roll(even[:, LANES:], N, 1))
        odd = jnp.where(low, pltpu.roll(odd[:, :LANES], N, 1), odd[:, LANES:])
        for start, value in ((2 * j, even + odd), (half * WIDE + 2 * j, even - odd)):
            by_ky[pl.ds(start, half, stride=WIDE), :] = value[:half]
            by_ky[pl.ds(start + 1, half, stride=WIDE), :] = value[half:]
    for place in range(N):
        first, zl = place // 16 * 16 + place % 4, place // 4 % 4
        rows = [by_ky[pl.ds((first + 4 * k) * WIDE + 8 * zl, 8), :] for k in range(4)]
        out_ref[place] = jnp.concatenate(rows, axis=0).astype(bf16)


def weight_row(fact_ref):
    lane = lane_index((1, LANES))
    chosen = jnp.where(lane.astype(f32) == fact_ref[0:1, :], fact_ref[3:4, :], 0.0)
    filled = jnp.sum(chosen, axis=1, keepdims=True)
    weight = (2.0 * (fact_ref[4:5, :] - filled) / fact_ref[5:6, :])[:, :BANDS]
    band = lax.broadcasted_iota(jnp.int32, (BANDS, LANES), 0).astype(f32)
    pick = jnp.where(band == fact_ref[1:2, :] + (lane % 8).astype(f32), 1.0, 0.0)
    return jnp.dot(weight, pick, precision=lax.Precision.HIGHEST, preferred_element_type=f32)


def spots_kernel(r_ref, e_ref, p_ref, fact_ref, out_ref, planes):
    for x in range(N):
        planes[pl.ds(x * WIDE, 32), :] = r_ref[x].astype(f32)
    column = lane_index((2 * LANES, LANES))
    band = lax.broadcasted_iota(jnp.int32, (2 * LANES, LANES), 0) // N
    total = jnp.zeros((2 * SPOTS, LANES), f32)
    for g in range(4):
        table = jnp.concatenate([e_ref[g, :, :LANES], e_ref[g, :, LANES:]], axis=0)
        cos_z = jnp.concatenate([p_ref[g, :, :LANES].astype(f32)] * 2, axis=1)
        sin_z = jnp.concatenate([p_ref[g, :, LANES:].astype(f32)] * 2, axis=1)
        for h in range(2):
            both = []
            for row in (8 * g + 4 * h, 8 * g + 4 * h + 2):
                parts = [planes[pl.ds(row + k, N, stride=WIDE), :] for k in range(2)]
                both.append(jnp.concatenate(parts, axis=0))
            first, second = both
            at_x = dot(table, jnp.concatenate([first, second], axis=1).astype(bf16))
            real, imag = at_x[:SPOTS], at_x[SPOTS:]
            real_z = real * cos_z + imag * sin_z
            imag_z = imag * cos_z - real * sin_z
            terms = jnp.concatenate([real_z, imag_z], axis=0).astype(bf16)
            ones = jnp.where(column == band + 16 * g + 4 * h, 1.0, 0.0).astype(bf16)
            total = total + dot(terms, ones)
    joined = total[:SPOTS] + pltpu.roll(total[SPOTS:], 8, 1)
    rows = (joined[:ROWS] * weight_row(fact_ref)).T
    for q in range(4):
        cols = joined[ROWS + 16 * q : ROWS + 16 * q + 16]
        cols = cols[:8] + pltpu.roll(cols[8:], N, 1)
        for g in range(4):
            block = [rows[16 * g : 16 * g + 16], cols, jnp.zeros_like(cols)]
            out_ref[4 * q + g] = jnp.concatenate(block, axis=0).astype(bf16)


def columns_kernel(v_ref, fact_ref, out_ref):
    second = fact_ref[2:3, :] > 0.5
    group = lane_index((32, LANES)) // 16
    rows = [jnp.zeros((32, LANES), f32)] * 4
    for s in range(8):
        core, zl = s // 4, s % 4
        cols = [v_ref[core, 4 * q + zl, 16:].astype(f32)[:8] for q in range(4)]
        cols = jnp.concatenate(cols, axis=0)
        cols = jnp.where(second, pltpu.roll(cols, N, 1), cols)
        for g in range(4):
            moved = cols if s == g else pltpu.roll(cols, 16 * (s - g) % LANES, 1)
            rows[g] = jnp.where(group == s, moved, rows[g])
    message = jnp.concatenate(rows, axis=0).astype(bf16)
    for i in range(16):
        out_ref[i] = message


def panel_kernel(a_ref, b_ref, out_ref, spread):
    for y in range(4):
        for x in range(4):
            for zl in range(4):
                at = (16 * y + 4 * zl + x) * WIDE
                spread[pl.ds(at, 32), :] = b_ref[4 * y + x, 32 * zl : 32 * zl + 32, :].astype(f32)
    real_lane = lane_index((ROWS, LANES)) % 16 < 8
    upper, lower = [], []
    for q in range(4):
        rows = [a_ref[s // 4, 4 * q + s % 4, :16].astype(f32) for s in range(8)]
        rows = jnp.concatenate(rows, axis=0).T
        turned = jnp.where(real_lane, pltpu.roll(rows, LANES - 8, 1), -pltpu.roll(rows, 8, 1))
        upper.append(rows.astype(bf16))
        lower.append(turned.astype(bf16))
    both = jnp.concatenate(
        [jnp.concatenate(upper, axis=1), jnp.concatenate(lower, axis=1)], axis=0
    )
    for h in range(2):
        columns = []
        for j in range(4 * h, 4 * h + 4):
            parts = [spread[pl.ds(8 * q + j, N, stride=WIDE), :] for q in range(4)]
            columns.append(jnp.concatenate(parts, axis=1))
        part = lax.dot_general(
            both,
            jnp.concatenate(columns, axis=0).astype(bf16),
            (((1,), (1,)), ((), ())),
            preferred_element_type=f32,
        )
        part = part * (1.0 / 16.0)
        out_ref[0, :, h * 256 : (h + 1) * 256] = part[:ROWS]
        out_ref[1, :, h * 256 : (h + 1) * 256] = part[ROWS:]


def call(kernel, shape, dtype, scratch, *args):
    vmem = pl.BlockSpec(memory_space=pltpu.VMEM)
    return pl.pallas_call(
        kernel,
        out_shape=jax.ShapeDtypeStruct(shape, dtype),
        in_specs=[vmem] * len(args),
        out_specs=vmem,
        scratch_shapes=scratch,
        compiler_params=pltpu.CompilerParams(vmem_limit_bytes=32 * 1024 * 1024),
    )(*args)


def shards(
    valence, conduction, band_index, occ_valence, occ_conduction, gap_energy, row_map, col_map
):
    chosen = band_index[0]
    core = lax.axis_index("c")
    local = lax.all_gather(valence.reshape(-1, N * N), "c", tiled=True)
    own = lax.dynamic_index_in_dim(local, chosen % local.shape[0], 0, keepdims=False)
    own = jnp.where(chosen // local.shape[0] == lax.axis_index("zh"), own, 0)
    v = lax.psum(own.astype(bf16).reshape(32, LANES), "zh")

    half = call(
        pair_y_kernel,
        (N, 32, LANES),
        bf16,
        [pltpu.VMEM((BANDS * WIDE, LANES), f32), pltpu.VMEM((N * WIDE, LANES), f32)],
        v,
        conduction.reshape(BANDS, N * N),
        jnp.asarray(y_table()).astype(bf16),
    )
    late = (half, row_map, col_map, occ_valence, occ_conduction, gap_energy)
    late = lax.optimization_barrier(late)
    half, row_map, col_map, occ_valence, occ_conduction, gap_energy = late
    block = lax.all_to_all(half, GA, 0, 0, tiled=True)

    mine = (jnp.arange(4) == lax.axis_index("zl"))[:, None]
    spots = jnp.where(mine, jnp.concatenate([row_map, col_map])[None], 0)
    spots = lax.psum(spots, "zl")
    grid = jnp.arange(N, dtype=jnp.int32)
    table = dot(((spots >> 6)[..., None] == grid).astype(bf16), jnp.asarray(x_table()).astype(bf16))
    phase = dot(((spots & 63)[..., None] == grid).astype(bf16), jnp.asarray(z_table()).astype(bf16))
    facts = [chosen, 8 * lax.axis_index("zl"), core]
    facts = [jnp.full((LANES,), fact) for fact in facts] + [occ_valence, jnp.tile(occ_conduction, 4)]
    facts = jnp.stack([fact.astype(f32) for fact in facts] + [jnp.tile(gap_energy, 4)])
    values = call(
        spots_kernel,
        (16, 32, LANES),
        bf16,
        [pltpu.VMEM((N * WIDE, LANES), f32)],
        block,
        table.astype(bf16),
        phase.astype(bf16),
        facts,
    )

    values = lax.all_to_all(values, ("zh", "zl"), 0, 0, tiled=True)
    values = lax.all_gather(values, "c")
    cols = call(
        columns_kernel,
        (16, ROWS, LANES),
        bf16,
        [],
        values,
        facts,
    )
    columns = lax.all_to_all(cols, ("y", "x"), 0, 0, tiled=True)
    return call(
        panel_kernel,
        (2, ROWS, 8 * N),
        f32,
        [pltpu.VMEM((N * WIDE, LANES), f32)],
        values,
        columns,
    )


def solution(mesh):
    fine = Mesh(mesh.devices.reshape(4, 4, 4, 4, 2), ("y", "zl", "x", "zh", "c"))
    return jax.shard_map(
        shards,
        mesh=fine,
        in_specs=(
            P(COL, GA, None),
            P(COL, GA, None),
            P(),
            P(),
            P(COL),
            P(COL),
            P(GA),
            P(GA),
        ),
        out_specs=P(None, GA, COL),
        check_vma=False,
    )
```

```python
import jax
import jax.numpy as jnp
import numpy as np
from jax import lax
from jax.experimental import pallas as pl
from jax.experimental.pallas import tpu as pltpu
from jax.sharding import Mesh
from jax.sharding import PartitionSpec as P

N = 64
BANDS = 32
ROWS = 128
COLS = 64
SPOTS = ROWS + COLS
LANES = 128
WIDE = 40
GA = ("y", "zl", "x")
COL = ("zh", "c")

f32 = jnp.float32
bf16 = jnp.bfloat16


def dot(left, right):
    return jnp.dot(left, right, preferred_element_type=f32)


def lane_index(shape):
    return lax.broadcasted_iota(jnp.int32, shape, len(shape) - 1)


def y_table():
    parity = np.arange(2)[:, None, None, None]
    imag = np.arange(2)[None, :, None, None]
    ky = np.arange(N // 2)[None, None, :, None]
    half = np.arange(N // 2)[None, None, None, :]
    turn = (ky * (2 * half + parity) + 16 * imag) % N
    return wave(turn).reshape(LANES, N // 2)


def wave(turn):
    return (np.cos(2.0 * np.pi * (turn % N) / N) / 8.0).astype(np.float32)


def x_table():
    kx = np.arange(N)[:, None]
    x, imag = np.arange(LANES)[None, :] % N, np.arange(LANES)[None, :] // N
    return np.concatenate([wave(kx * x - 16 * imag), wave(kx * x + 16 * (1 - imag))], axis=1)


def z_table():
    turn = np.arange(N)[:, None] * (np.arange(LANES)[None, :] % N)
    return np.concatenate([wave(turn), wave(turn - 16)], axis=1)


def pair_y_kernel(v_ref, c_ref, e_ref, out_ref, by_row, by_ky):
    v = v_ref[...].astype(f32)
    for i in range(N // 2):
        bands = c_ref[:, i * LANES : (i + 1) * LANES].astype(f32)
        pair = (bands * v[i : i + 1, :]).astype(bf16).astype(f32)
        by_row[pl.ds(i, BANDS, stride=WIDE), :] = pair
    table = e_ref[...]
    low = lane_index((N, LANES)) < N
    half = N // 2
    for j in range(BANDS // 2):
        first = by_row[pl.ds(2 * WIDE * j, half), :]
        second = by_row[pl.ds(2 * WIDE * j + WIDE, half), :]
        both = dot(table, jnp.concatenate([first, second], axis=1).astype(bf16))
        even, odd = both[:N], both[N:]
        even = jnp.where(low, even[:, :LANES], pltpu.roll(even[:, LANES:], N, 1))
        odd = jnp.where(low, pltpu.roll(odd[:, :LANES], N, 1), odd[:, LANES:])
        for start, value in ((2 * j, even + odd), (half * WIDE + 2 * j, even - odd)):
            by_ky[pl.ds(start, half, stride=WIDE), :] = value[:half]
            by_ky[pl.ds(start + 1, half, stride=WIDE), :] = value[half:]
    for place in range(N):
        first, zl = place // 16 * 16 + place % 4, place // 4 % 4
        rows = [by_ky[pl.ds((first + 4 * k) * WIDE + 8 * zl, 8), :] for k in range(4)]
        out_ref[place] = jnp.concatenate(rows, axis=0).astype(bf16)


def weight_row(fact_ref):
    lane = lane_index((1, LANES))
    chosen = jnp.where(lane.astype(f32) == fact_ref[0:1, :], fact_ref[3:4, :], 0.0)
    filled = jnp.sum(chosen, axis=1, keepdims=True)
    weight = (2.0 * (fact_ref[4:5, :] - filled) / fact_ref[5:6, :])[:, :BANDS]
    band = lax.broadcasted_iota(jnp.int32, (BANDS, LANES), 0).astype(f32)
    pick = jnp.where(band == fact_ref[1:2, :] + (lane % 8).astype(f32), 1.0, 0.0)
    return jnp.dot(weight, pick, precision=lax.Precision.HIGHEST, preferred_element_type=f32)


def spots_kernel(r_ref, e_ref, p_ref, fact_ref, out_ref, planes):
    for x in range(N):
        planes[pl.ds(x * WIDE, 32), :] = r_ref[x].astype(f32)
    column = lane_index((2 * LANES, LANES))
    band = lax.broadcasted_iota(jnp.int32, (2 * LANES, LANES), 0) // N
    total = jnp.zeros((2 * SPOTS, LANES), f32)
    for g in range(4):
        table = jnp.concatenate([e_ref[g, :, :LANES], e_ref[g, :, LANES:]], axis=0)
        cos_z = jnp.concatenate([p_ref[g, :, :LANES].astype(f32)] * 2, axis=1)
        sin_z = jnp.concatenate([p_ref[g, :, LANES:].astype(f32)] * 2, axis=1)
        for h in range(2):
            both = []
            for row in (8 * g + 4 * h, 8 * g + 4 * h + 2):
                parts = [planes[pl.ds(row + k, N, stride=WIDE), :] for k in range(2)]
                both.append(jnp.concatenate(parts, axis=0))
            first, second = both
            at_x = dot(table, jnp.concatenate([first, second], axis=1).astype(bf16))
            real, imag = at_x[:SPOTS], at_x[SPOTS:]
            real_z = real * cos_z + imag * sin_z
            imag_z = imag * cos_z - real * sin_z
            terms = jnp.concatenate([real_z, imag_z], axis=0).astype(bf16)
            ones = jnp.where(column == band + 16 * g + 4 * h, 1.0, 0.0).astype(bf16)
            total = total + dot(terms, ones)
    joined = total[:SPOTS] + pltpu.roll(total[SPOTS:], 8, 1)
    rows = (joined[:ROWS] * weight_row(fact_ref)).T
    for q in range(4):
        cols = joined[ROWS + 16 * q : ROWS + 16 * q + 16]
        cols = cols[:8] + pltpu.roll(cols[8:], N, 1)
        for g in range(4):
            block = [rows[16 * g : 16 * g + 16], cols]
            out_ref[4 * q + g] = jnp.concatenate(block, axis=0).astype(bf16)


def columns_kernel(v_ref, fact_ref, out_ref):
    second = fact_ref[2:3, :] > 0.5
    group = lane_index((32, LANES)) // 16
    rows = [jnp.zeros((32, LANES), f32)] * 4
    for s in range(8):
        core, zl = s // 4, s % 4
        cols = [v_ref[core, 4 * q + zl].astype(f32)[16:] for q in range(4)]
        cols = jnp.concatenate(cols, axis=0)
        cols = jnp.where(second, pltpu.roll(cols, N, 1), cols)
        for g in range(4):
            moved = cols if s == g else pltpu.roll(cols, 16 * (s - g) % LANES, 1)
            rows[g] = jnp.where(group == s, moved, rows[g])
    message = jnp.concatenate(rows, axis=0).astype(bf16)
    for i in range(16):
        out_ref[i] = message


def panel_kernel(a_ref, b_ref, out_ref, spread):
    for y in range(4):
        for x in range(4):
            for zl in range(4):
                at = (16 * y + 4 * zl + x) * WIDE
                spread[pl.ds(at, 32), :] = b_ref[4 * x + y, 32 * zl : 32 * zl + 32, :].astype(f32)
    real_lane = lane_index((ROWS, LANES)) % 16 < 8
    upper, lower = [], []
    for q in range(4):
        rows = [a_ref[s // 4, 4 * q + s % 4].astype(f32)[:16] for s in range(8)]
        rows = jnp.concatenate(rows, axis=0).T
        turned = jnp.where(real_lane, pltpu.roll(rows, LANES - 8, 1), -pltpu.roll(rows, 8, 1))
        upper.append(rows.astype(bf16))
        lower.append(turned.astype(bf16))
    both = jnp.concatenate(
        [jnp.concatenate(upper, axis=1), jnp.concatenate(lower, axis=1)], axis=0
    )
    for h in range(2):
        columns = []
        for j in range(4 * h, 4 * h + 4):
            parts = [spread[pl.ds(8 * q + j, N, stride=WIDE), :] for q in range(4)]
            columns.append(jnp.concatenate(parts, axis=1))
        part = lax.dot_general(
            both,
            jnp.concatenate(columns, axis=0).astype(bf16),
            (((1,), (1,)), ((), ())),
            preferred_element_type=f32,
        )
        part = part * (1.0 / 16.0)
        out_ref[0, :, h * 256 : (h + 1) * 256] = part[:ROWS]
        out_ref[1, :, h * 256 : (h + 1) * 256] = part[ROWS:]


def call(kernel, shape, dtype, scratch, *args):
    vmem = pl.BlockSpec(memory_space=pltpu.VMEM)
    return pl.pallas_call(
        kernel,
        out_shape=jax.ShapeDtypeStruct(shape, dtype),
        in_specs=[vmem] * len(args),
        out_specs=vmem,
        scratch_shapes=scratch,
        compiler_params=pltpu.CompilerParams(vmem_limit_bytes=32 * 1024 * 1024),
    )(*args)


def shards(
    valence, conduction, band_index, occ_valence, occ_conduction, gap_energy, row_map, col_map
):
    chosen = band_index[0]
    core = lax.axis_index("c")
    local = lax.all_gather(valence.reshape(-1, N * N), "c", tiled=True)
    band = lax.broadcasted_iota(jnp.int32, local.shape, 0) + local.shape[0] * lax.axis_index("zh")
    own = jnp.sum(jnp.where(band == band_index, local, 0).astype(f32), axis=0)
    v = lax.psum(own.astype(bf16).reshape(32, LANES), "zh")

    half = call(
        pair_y_kernel,
        (N, 32, LANES),
        bf16,
        [pltpu.VMEM((BANDS * WIDE, LANES), f32), pltpu.VMEM((N * WIDE, LANES), f32)],
        v,
        conduction.reshape(BANDS, N * N),
        jnp.asarray(y_table()).astype(bf16),
    )
    late = (half, row_map, col_map, occ_valence, occ_conduction, gap_energy)
    late = lax.optimization_barrier(late)
    half, row_map, col_map, occ_valence, occ_conduction, gap_energy = late
    block = lax.all_to_all(half, GA, 0, 0, tiled=True)

    mine = (jnp.arange(4) == lax.axis_index("zl"))[:, None]
    spots = jnp.where(mine, jnp.concatenate([row_map, col_map])[None], 0)
    spots = lax.psum(spots, "zl")
    grid = jnp.arange(N, dtype=jnp.int32)
    table = dot(((spots >> 6)[..., None] == grid).astype(bf16), jnp.asarray(x_table()).astype(bf16))
    phase = dot(((spots & 63)[..., None] == grid).astype(bf16), jnp.asarray(z_table()).astype(bf16))
    facts = [chosen, 8 * lax.axis_index("zl"), core]
    facts = [jnp.full((LANES,), fact) for fact in facts] + [occ_valence, jnp.tile(occ_conduction, 4)]
    facts = jnp.stack([fact.astype(f32) for fact in facts] + [jnp.tile(gap_energy, 4)])
    values = call(
        spots_kernel,
        (16, 24, LANES),
        bf16,
        [pltpu.VMEM((N * WIDE, LANES), f32)],
        block,
        table.astype(bf16),
        phase.astype(bf16),
        facts,
    )

    values = lax.all_to_all(values, ("zh", "zl"), 0, 0, tiled=True)
    values = lax.all_gather(values, "c")
    cols = call(
        columns_kernel,
        (16, ROWS, LANES),
        bf16,
        [],
        values,
        facts,
    )
    columns = lax.all_to_all(cols, ("x", "y"), 0, 0, tiled=True)
    return call(
        panel_kernel,
        (2, ROWS, 8 * N),
        f32,
        [pltpu.VMEM((N * WIDE, LANES), f32)],
        values,
        columns,
    )


def solution(mesh):
    fine = Mesh(mesh.devices.reshape(4, 4, 4, 4, 2), ("y", "zl", "x", "zh", "c"))
    return jax.shard_map(
        shards,
        mesh=fine,
        in_specs=(
            P(COL, GA, None),
            P(COL, GA, None),
            P(),
            P(),
            P(COL),
            P(COL),
            P(GA),
            P(GA),
        ),
        out_specs=P(None, GA, COL),
        check_vma=False,
    )
```

```python
import jax
import jax.numpy as jnp
import numpy as np
from jax import lax
from jax.experimental import pallas as pl
from jax.experimental.pallas import tpu as pltpu
from jax.sharding import Mesh
from jax.sharding import PartitionSpec as P

N = 64
BANDS = 32
ROWS = 128
COLS = 64
SPOTS = ROWS + COLS
LANES = 128
WIDE = 40
GA = ("y", "zl", "x")
COL = ("zh", "c")

f32 = jnp.float32
bf16 = jnp.bfloat16


def dot(left, right):
    return jnp.dot(left, right, preferred_element_type=f32)


def lane_index(shape):
    return lax.broadcasted_iota(jnp.int32, shape, len(shape) - 1)


def y_table():
    parity = np.arange(2)[:, None, None, None]
    imag = np.arange(2)[None, :, None, None]
    ky = np.arange(N // 2)[None, None, :, None]
    half = np.arange(N // 2)[None, None, None, :]
    turn = (ky * (2 * half + parity) + 16 * imag) % N
    return wave(turn).reshape(LANES, N // 2)


def wave(turn):
    return (np.cos(2.0 * np.pi * (turn % N) / N) / 8.0).astype(np.float32)


def x_table():
    kx = np.arange(N)[:, None]
    x, imag = np.arange(LANES)[None, :] % N, np.arange(LANES)[None, :] // N
    return np.concatenate([wave(kx * x - 16 * imag), wave(kx * x + 16 * (1 - imag))], axis=1)


def z_table():
    turn = np.arange(N)[:, None] * (np.arange(LANES)[None, :] % N)
    return np.concatenate([wave(turn), wave(turn - 16)], axis=1)


def pair_y_kernel(v_ref, c_ref, e_ref, out_hbm, by_row, by_ky, out_ref, sent):
    v = v_ref[...].astype(f32)
    for i in range(N // 2):
        bands = c_ref[:, i * LANES : (i + 1) * LANES].astype(f32)
        pair = (bands * v[i : i + 1, :]).astype(bf16).astype(f32)
        by_row[pl.ds(i, BANDS, stride=WIDE), :] = pair
    table = e_ref[...]
    low = lane_index((N, LANES)) < N
    half = N // 2
    for j in range(BANDS // 2):
        first = by_row[pl.ds(2 * WIDE * j, half), :]
        second = by_row[pl.ds(2 * WIDE * j + WIDE, half), :]
        both = dot(table, jnp.concatenate([first, second], axis=1).astype(bf16))
        even, odd = both[:N], both[N:]
        even = jnp.where(low, even[:, :LANES], pltpu.roll(even[:, LANES:], N, 1))
        odd = jnp.where(low, pltpu.roll(odd[:, :LANES], N, 1), odd[:, LANES:])
        for start, value in ((2 * j, even + odd), (half * WIDE + 2 * j, even - odd)):
            by_ky[pl.ds(start, half, stride=WIDE), :] = value[:half]
            by_ky[pl.ds(start + 1, half, stride=WIDE), :] = value[half:]
    copies = []
    for place in range(N):
        first, zl = place // 16 * 16 + place % 4, place // 4 % 4
        rows = [by_ky[pl.ds((first + 4 * k) * WIDE + 8 * zl, 8), :] for k in range(4)]
        out_ref[place] = jnp.concatenate(rows, axis=0).astype(bf16)
        if place % 16 == 15:
            part = pl.ds(place - 15, 16)
            copies.append(pltpu.make_async_copy(out_ref.at[part], out_hbm.at[part], sent.at[place // 16]))
            copies[-1].start()
    for copy in copies:
        copy.wait()


def weight_row(fact_ref):
    lane = lane_index((1, LANES))
    chosen = jnp.where(lane.astype(f32) == fact_ref[0:1, :], fact_ref[3:4, :], 0.0)
    filled = jnp.sum(chosen, axis=1, keepdims=True)
    weight = (2.0 * (fact_ref[4:5, :] - filled) / fact_ref[5:6, :])[:, :BANDS]
    band = lax.broadcasted_iota(jnp.int32, (BANDS, LANES), 0).astype(f32)
    pick = jnp.where(band == fact_ref[1:2, :] + (lane % 8).astype(f32), 1.0, 0.0)
    return jnp.dot(weight, pick, precision=lax.Precision.HIGHEST, preferred_element_type=f32)


def spots_kernel(r_ref, e_ref, p_ref, fact_ref, out_ref, planes):
    for x in range(N):
        planes[pl.ds(x * WIDE, 32), :] = r_ref[x].astype(f32)
    column = lane_index((2 * LANES, LANES))
    band = lax.broadcasted_iota(jnp.int32, (2 * LANES, LANES), 0) // N
    total = jnp.zeros((2 * SPOTS, LANES), f32)
    for g in range(4):
        table = jnp.concatenate([e_ref[g, :, :LANES], e_ref[g, :, LANES:]], axis=0)
        cos_z = jnp.concatenate([p_ref[g, :, :LANES].astype(f32)] * 2, axis=1)
        sin_z = jnp.concatenate([p_ref[g, :, LANES:].astype(f32)] * 2, axis=1)
        for h in range(2):
            both = []
            for row in (8 * g + 4 * h, 8 * g + 4 * h + 2):
                parts = [planes[pl.ds(row + k, N, stride=WIDE), :] for k in range(2)]
                both.append(jnp.concatenate(parts, axis=0))
            first, second = both
            at_x = dot(table, jnp.concatenate([first, second], axis=1).astype(bf16))
            real, imag = at_x[:SPOTS], at_x[SPOTS:]
            real_z = real * cos_z + imag * sin_z
            imag_z = imag * cos_z - real * sin_z
            terms = jnp.concatenate([real_z, imag_z], axis=0).astype(bf16)
            ones = jnp.where(column == band + 16 * g + 4 * h, 1.0, 0.0).astype(bf16)
            total = total + dot(terms, ones)
    joined = total[:SPOTS] + pltpu.roll(total[SPOTS:], 8, 1)
    rows = (joined[:ROWS] * weight_row(fact_ref)).T
    for q in range(4):
        cols = joined[ROWS + 16 * q : ROWS + 16 * q + 16]
        cols = cols[:8] + pltpu.roll(cols[8:], N, 1)
        for g in range(4):
            block = [rows[16 * g : 16 * g + 16], cols]
            out_ref[4 * q + g] = jnp.concatenate(block, axis=0).astype(bf16)


def columns_kernel(v_ref, fact_ref, out_ref):
    second = fact_ref[2:3, :] > 0.5
    group = lane_index((32, LANES)) // 16
    rows = [jnp.zeros((32, LANES), f32)] * 4
    for s in range(8):
        core, zl = s // 4, s % 4
        cols = [v_ref[core, 4 * q + zl].astype(f32)[16:] for q in range(4)]
        cols = jnp.concatenate(cols, axis=0)
        cols = jnp.where(second, pltpu.roll(cols, N, 1), cols)
        for g in range(4):
            moved = cols if s == g else pltpu.roll(cols, 16 * (s - g) % LANES, 1)
            rows[g] = jnp.where(group == s, moved, rows[g])
    message = jnp.concatenate(rows, axis=0).astype(bf16)
    for i in range(16):
        out_ref[i] = message


def panel_kernel(a_ref, b_ref, out_ref, spread):
    for y in range(4):
        for x in range(4):
            for zl in range(4):
                at = (16 * y + 4 * zl + x) * WIDE
                spread[pl.ds(at, 32), :] = b_ref[4 * x + y, 32 * zl : 32 * zl + 32, :].astype(f32)
    real_lane = lane_index((ROWS, LANES)) % 16 < 8
    upper, lower = [], []
    for q in range(4):
        rows = [a_ref[s // 4, 4 * q + s % 4].astype(f32)[:16] for s in range(8)]
        rows = jnp.concatenate(rows, axis=0).T
        turned = jnp.where(real_lane, pltpu.roll(rows, LANES - 8, 1), -pltpu.roll(rows, 8, 1))
        upper.append(rows.astype(bf16))
        lower.append(turned.astype(bf16))
    both = jnp.concatenate(
        [jnp.concatenate(upper, axis=1), jnp.concatenate(lower, axis=1)], axis=0
    )
    for h in range(2):
        columns = []
        for j in range(4 * h, 4 * h + 4):
            parts = [spread[pl.ds(8 * q + j, N, stride=WIDE), :] for q in range(4)]
            columns.append(jnp.concatenate(parts, axis=1))
        part = lax.dot_general(
            both,
            jnp.concatenate(columns, axis=0).astype(bf16),
            (((1,), (1,)), ((), ())),
            preferred_element_type=f32,
        )
        part = part * (1.0 / 16.0)
        out_ref[0, :, h * 256 : (h + 1) * 256] = part[:ROWS]
        out_ref[1, :, h * 256 : (h + 1) * 256] = part[ROWS:]


def call(kernel, shape, dtype, scratch, *args, out_space=pltpu.VMEM):
    vmem = pl.BlockSpec(memory_space=pltpu.VMEM)
    return pl.pallas_call(
        kernel,
        out_shape=jax.ShapeDtypeStruct(shape, dtype),
        in_specs=[vmem] * len(args),
        out_specs=pl.BlockSpec(memory_space=out_space),
        scratch_shapes=scratch,
        compiler_params=pltpu.CompilerParams(vmem_limit_bytes=32 * 1024 * 1024),
    )(*args)


def shards(
    valence, conduction, band_index, occ_valence, occ_conduction, gap_energy, row_map, col_map
):
    chosen = band_index[0]
    core = lax.axis_index("c")
    local = lax.all_gather(valence.reshape(-1, N * N), "c", tiled=True)
    band = lax.broadcasted_iota(jnp.int32, local.shape, 0) + local.shape[0] * lax.axis_index("zh")
    own = jnp.sum(jnp.where(band == band_index, local, 0).astype(f32), axis=0)
    v = lax.psum(own.astype(bf16).reshape(32, LANES), "zh")

    half = call(
        pair_y_kernel,
        (N, 32, LANES),
        bf16,
        [
            pltpu.VMEM((BANDS * WIDE, LANES), f32),
            pltpu.VMEM((N * WIDE, LANES), f32),
            pltpu.VMEM((N, 32, LANES), bf16),
            pltpu.SemaphoreType.DMA((4,)),
        ],
        v,
        conduction.reshape(BANDS, N * N),
        jnp.asarray(y_table()).astype(bf16),
        out_space=pl.ANY,
    )
    late = (half, row_map, col_map, occ_valence, occ_conduction, gap_energy)
    late = lax.optimization_barrier(late)
    half, row_map, col_map, occ_valence, occ_conduction, gap_energy = late
    block = lax.all_to_all(half, GA, 0, 0, tiled=True)

    mine = (jnp.arange(4) == lax.axis_index("zl"))[:, None]
    spots = jnp.where(mine, jnp.concatenate([row_map, col_map])[None], 0)
    spots = lax.psum(spots, "zl")
    grid = jnp.arange(N, dtype=jnp.int32)
    table = dot(((spots >> 6)[..., None] == grid).astype(bf16), jnp.asarray(x_table()).astype(bf16))
    phase = dot(((spots & 63)[..., None] == grid).astype(bf16), jnp.asarray(z_table()).astype(bf16))
    facts = [chosen, 8 * lax.axis_index("zl"), core]
    facts = [jnp.full((LANES,), fact) for fact in facts] + [occ_valence, jnp.tile(occ_conduction, 4)]
    facts = jnp.stack([fact.astype(f32) for fact in facts] + [jnp.tile(gap_energy, 4)])
    values = call(
        spots_kernel,
        (16, 24, LANES),
        bf16,
        [pltpu.VMEM((N * WIDE, LANES), f32)],
        block,
        table.astype(bf16),
        phase.astype(bf16),
        facts,
    )

    values = lax.all_to_all(values, ("zh", "zl"), 0, 0, tiled=True)
    values = lax.all_gather(values, "c")
    cols = call(
        columns_kernel,
        (16, ROWS, LANES),
        bf16,
        [],
        values,
        facts,
    )
    columns = lax.all_to_all(cols, ("x", "y"), 0, 0, tiled=True)
    return call(
        panel_kernel,
        (2, ROWS, 8 * N),
        f32,
        [pltpu.VMEM((N * WIDE, LANES), f32)],
        values,
        columns,
    )


def solution(mesh):
    fine = Mesh(mesh.devices.reshape(4, 4, 4, 4, 2), ("y", "zl", "x", "zh", "c"))
    return jax.shard_map(
        shards,
        mesh=fine,
        in_specs=(
            P(COL, GA, None),
            P(COL, GA, None),
            P(),
            P(),
            P(COL),
            P(COL),
            P(GA),
            P(GA),
        ),
        out_specs=P(None, GA, COL),
        check_vma=False,
    )
```

```python
import jax
import jax.numpy as jnp
import numpy as np
from jax import lax
from jax.experimental import pallas as pl
from jax.experimental.pallas import tpu as pltpu
from jax.sharding import Mesh
from jax.sharding import PartitionSpec as P

N = 64
BANDS = 32
ROWS = 128
COLS = 64
SPOTS = ROWS + COLS
LANES = 128
WIDE = 40
GA = ("y", "zl", "x")
COL = ("zh", "c")

f32 = jnp.float32
bf16 = jnp.bfloat16


def dot(left, right):
    return jnp.dot(left, right, preferred_element_type=f32)


def lane_index(shape):
    return lax.broadcasted_iota(jnp.int32, shape, len(shape) - 1)


def y_table():
    parity = np.arange(2)[:, None, None, None]
    imag = np.arange(2)[None, :, None, None]
    ky = np.arange(N // 2)[None, None, :, None]
    half = np.arange(N // 2)[None, None, None, :]
    turn = (ky * (2 * half + parity) + 16 * imag) % N
    return wave(turn).reshape(LANES, N // 2)


def wave(turn):
    return (np.cos(2.0 * np.pi * (turn % N) / N) / 8.0).astype(np.float32)


def x_table():
    kx = np.arange(N)[:, None]
    x, imag = np.arange(LANES)[None, :] % N, np.arange(LANES)[None, :] // N
    return np.concatenate([wave(kx * x - 16 * imag), wave(kx * x + 16 * (1 - imag))], axis=1)


def z_table():
    turn = np.arange(N)[:, None] * (np.arange(LANES)[None, :] % N)
    return np.concatenate([wave(turn), wave(turn - 16)], axis=1)


def pair_y_kernel(v_ref, c_ref, e_ref, out_hbm, by_row, by_ky, out_ref, sent):
    v = v_ref[...].astype(f32)
    for i in range(N // 2):
        bands = c_ref[:, i * LANES : (i + 1) * LANES].astype(f32)
        pair = (bands * v[i : i + 1, :]).astype(bf16).astype(f32)
        by_row[pl.ds(i, BANDS, stride=WIDE), :] = pair
    table = e_ref[...]
    low = lane_index((N, LANES)) < N
    half = N // 2
    for j in range(BANDS // 2):
        first = by_row[pl.ds(2 * WIDE * j, half), :]
        second = by_row[pl.ds(2 * WIDE * j + WIDE, half), :]
        both = dot(table, jnp.concatenate([first, second], axis=1).astype(bf16))
        even, odd = both[:N], both[N:]
        even = jnp.where(low, even[:, :LANES], pltpu.roll(even[:, LANES:], N, 1))
        odd = jnp.where(low, pltpu.roll(odd[:, :LANES], N, 1), odd[:, LANES:])
        for start, value in ((2 * j, even + odd), (half * WIDE + 2 * j, even - odd)):
            by_ky[pl.ds(start, half, stride=WIDE), :] = value[:half]
            by_ky[pl.ds(start + 1, half, stride=WIDE), :] = value[half:]
    copies = []
    for place in range(N):
        first, zl = place // 4 % 4 * 16 + place % 4, place // 16
        rows = [by_ky[pl.ds((first + 4 * k) * WIDE + 8 * zl, 8), :] for k in range(4)]
        out_ref[place] = jnp.concatenate(rows, axis=0).astype(bf16)
        if place % 16 == 15:
            part = pl.ds(place - 15, 16)
            copies.append(pltpu.make_async_copy(out_ref.at[part], out_hbm.at[part], sent.at[place // 16]))
            copies[-1].start()
    for copy in copies:
        copy.wait()


def weight_row(fact_ref):
    lane = lane_index((1, LANES))
    chosen = jnp.where(lane.astype(f32) == fact_ref[0:1, :], fact_ref[3:4, :], 0.0)
    filled = jnp.sum(chosen, axis=1, keepdims=True)
    weight = (2.0 * (fact_ref[4:5, :] - filled) / fact_ref[5:6, :])[:, :BANDS]
    band = lax.broadcasted_iota(jnp.int32, (BANDS, LANES), 0).astype(f32)
    pick = jnp.where(band == fact_ref[1:2, :] + (lane % 8).astype(f32), 1.0, 0.0)
    return jnp.dot(weight, pick, precision=lax.Precision.HIGHEST, preferred_element_type=f32)


def spots_kernel(r_ref, e_ref, p_ref, fact_ref, out_ref, planes):
    for x in range(N):
        place = x // 4 % 4 * 16 + x // 16 * 4 + x % 4
        planes[pl.ds(x * WIDE, 32), :] = r_ref[place].astype(f32)
    column = lane_index((2 * LANES, LANES))
    band = lax.broadcasted_iota(jnp.int32, (2 * LANES, LANES), 0) // N
    total = jnp.zeros((2 * SPOTS, LANES), f32)
    for g in range(4):
        table = jnp.concatenate([e_ref[g, :, :LANES], e_ref[g, :, LANES:]], axis=0)
        cos_z = jnp.concatenate([p_ref[g, :, :LANES].astype(f32)] * 2, axis=1)
        sin_z = jnp.concatenate([p_ref[g, :, LANES:].astype(f32)] * 2, axis=1)
        for h in range(2):
            both = []
            for row in (8 * g + 4 * h, 8 * g + 4 * h + 2):
                parts = [planes[pl.ds(row + k, N, stride=WIDE), :] for k in range(2)]
                both.append(jnp.concatenate(parts, axis=0))
            first, second = both
            at_x = dot(table, jnp.concatenate([first, second], axis=1).astype(bf16))
            real, imag = at_x[:SPOTS], at_x[SPOTS:]
            real_z = real * cos_z + imag * sin_z
            imag_z = imag * cos_z - real * sin_z
            terms = jnp.concatenate([real_z, imag_z], axis=0).astype(bf16)
            ones = jnp.where(column == band + 16 * g + 4 * h, 1.0, 0.0).astype(bf16)
            total = total + dot(terms, ones)
    joined = total[:SPOTS] + pltpu.roll(total[SPOTS:], 8, 1)
    rows = (joined[:ROWS] * weight_row(fact_ref)).T
    for q in range(4):
        cols = joined[ROWS + 16 * q : ROWS + 16 * q + 16]
        cols = cols[:8] + pltpu.roll(cols[8:], N, 1)
        for g in range(4):
            block = [rows[16 * g : 16 * g + 16], cols]
            out_ref[4 * q + g] = jnp.concatenate(block, axis=0).astype(bf16)


def columns_kernel(v_ref, fact_ref, out_ref):
    second = fact_ref[2:3, :] > 0.5
    group = lane_index((32, LANES)) // 16
    rows = [jnp.zeros((32, LANES), f32)] * 4
    for s in range(8):
        core, zl = s // 4, s % 4
        cols = [v_ref[core, 4 * q + zl].astype(f32)[16:] for q in range(4)]
        cols = jnp.concatenate(cols, axis=0)
        cols = jnp.where(second, pltpu.roll(cols, N, 1), cols)
        for g in range(4):
            moved = cols if s == g else pltpu.roll(cols, 16 * (s - g) % LANES, 1)
            rows[g] = jnp.where(group == s, moved, rows[g])
    message = jnp.concatenate(rows, axis=0).astype(bf16)
    for i in range(16):
        out_ref[i] = message


def panel_kernel(a_ref, b_ref, out_ref, spread):
    for y in range(4):
        for x in range(4):
            for zl in range(4):
                at = (16 * y + 4 * zl + x) * WIDE
                spread[pl.ds(at, 32), :] = b_ref[4 * x + y, 32 * zl : 32 * zl + 32, :].astype(f32)
    real_lane = lane_index((ROWS, LANES)) % 16 < 8
    upper, lower = [], []
    for q in range(4):
        rows = [a_ref[s // 4, 4 * q + s % 4].astype(f32)[:16] for s in range(8)]
        rows = jnp.concatenate(rows, axis=0).T
        turned = jnp.where(real_lane, pltpu.roll(rows, LANES - 8, 1), -pltpu.roll(rows, 8, 1))
        upper.append(rows.astype(bf16))
        lower.append(turned.astype(bf16))
    both = jnp.concatenate(
        [jnp.concatenate(upper, axis=1), jnp.concatenate(lower, axis=1)], axis=0
    )
    for h in range(2):
        columns = []
        for j in range(4 * h, 4 * h + 4):
            parts = [spread[pl.ds(8 * q + j, N, stride=WIDE), :] for q in range(4)]
            columns.append(jnp.concatenate(parts, axis=1))
        part = lax.dot_general(
            both,
            jnp.concatenate(columns, axis=0).astype(bf16),
            (((1,), (1,)), ((), ())),
            preferred_element_type=f32,
        )
        part = part * (1.0 / 16.0)
        out_ref[0, :, h * 256 : (h + 1) * 256] = part[:ROWS]
        out_ref[1, :, h * 256 : (h + 1) * 256] = part[ROWS:]


def call(kernel, shape, dtype, scratch, *args, out_space=pltpu.VMEM):
    vmem = pl.BlockSpec(memory_space=pltpu.VMEM)
    return pl.pallas_call(
        kernel,
        out_shape=jax.ShapeDtypeStruct(shape, dtype),
        in_specs=[vmem] * len(args),
        out_specs=pl.BlockSpec(memory_space=out_space),
        scratch_shapes=scratch,
        compiler_params=pltpu.CompilerParams(vmem_limit_bytes=32 * 1024 * 1024),
    )(*args)


def shards(
    valence, conduction, band_index, occ_valence, occ_conduction, gap_energy, row_map, col_map
):
    chosen = band_index[0]
    core = lax.axis_index("c")
    local = lax.all_gather(valence.reshape(-1, N * N), "c", tiled=True)
    band = lax.broadcasted_iota(jnp.int32, local.shape, 0) + local.shape[0] * lax.axis_index("zh")
    own = jnp.sum(jnp.where(band == band_index, local, 0).astype(f32), axis=0)
    v = lax.psum(own.astype(bf16).reshape(32, LANES), "zh")

    half = call(
        pair_y_kernel,
        (N, 32, LANES),
        bf16,
        [
            pltpu.VMEM((BANDS * WIDE, LANES), f32),
            pltpu.VMEM((N * WIDE, LANES), f32),
            pltpu.VMEM((N, 32, LANES), bf16),
            pltpu.SemaphoreType.DMA((4,)),
        ],
        v,
        conduction.reshape(BANDS, N * N),
        jnp.asarray(y_table()).astype(bf16),
        out_space=pl.ANY,
    )
    late = (half, row_map, col_map, occ_valence, occ_conduction, gap_energy)
    late = lax.optimization_barrier(late)
    half, row_map, col_map, occ_valence, occ_conduction, gap_energy = late
    block = lax.all_to_all(half, ("zl", "y", "x"), 0, 0, tiled=True)

    mine = (jnp.arange(4) == lax.axis_index("zl"))[:, None]
    spots = jnp.where(mine, jnp.concatenate([row_map, col_map])[None], 0)
    spots = lax.psum(spots, "zl")
    grid = jnp.arange(N, dtype=jnp.int32)
    table = dot(((spots >> 6)[..., None] == grid).astype(bf16), jnp.asarray(x_table()).astype(bf16))
    phase = dot(((spots & 63)[..., None] == grid).astype(bf16), jnp.asarray(z_table()).astype(bf16))
    facts = [chosen, 8 * lax.axis_index("zl"), core]
    facts = [jnp.full((LANES,), fact) for fact in facts] + [occ_valence, jnp.tile(occ_conduction, 4)]
    facts = jnp.stack([fact.astype(f32) for fact in facts] + [jnp.tile(gap_energy, 4)])
    values = call(
        spots_kernel,
        (16, 24, LANES),
        bf16,
        [pltpu.VMEM((N * WIDE, LANES), f32)],
        block,
        table.astype(bf16),
        phase.astype(bf16),
        facts,
    )

    values = lax.all_to_all(values, ("zh", "zl"), 0, 0, tiled=True)
    values = lax.all_gather(values, "c")
    cols = call(
        columns_kernel,
        (16, ROWS, LANES),
        bf16,
        [],
        values,
        facts,
    )
    columns = lax.all_to_all(cols, ("x", "y"), 0, 0, tiled=True)
    return call(
        panel_kernel,
        (2, ROWS, 8 * N),
        f32,
        [pltpu.VMEM((N * WIDE, LANES), f32)],
        values,
        columns,
    )


def solution(mesh):
    fine = Mesh(mesh.devices.reshape(4, 4, 4, 4, 2), ("y", "zl", "x", "zh", "c"))
    return jax.shard_map(
        shards,
        mesh=fine,
        in_specs=(
            P(COL, GA, None),
            P(COL, GA, None),
            P(),
            P(),
            P(COL),
            P(COL),
            P(GA),
            P(GA),
        ),
        out_specs=P(None, GA, COL),
        check_vma=False,
    )
```

```python
import jax
import jax.numpy as jnp
import numpy as np
from jax import lax
from jax.experimental import pallas as pl
from jax.experimental.pallas import tpu as pltpu
from jax.sharding import Mesh
from jax.sharding import PartitionSpec as P

N = 64
BANDS = 32
ROWS = 128
COLS = 64
SPOTS = ROWS + COLS
LANES = 128
WIDE = 40
GA = ("y", "zl", "x")
COL = ("zh", "c")

f32 = jnp.float32
bf16 = jnp.bfloat16


def dot(left, right):
    return jnp.dot(left, right, preferred_element_type=f32)


def lane_index(shape):
    return lax.broadcasted_iota(jnp.int32, shape, len(shape) - 1)


def y_table():
    parity = np.arange(2)[:, None, None, None]
    imag = np.arange(2)[None, :, None, None]
    ky = np.arange(N // 2)[None, None, :, None]
    half = np.arange(N // 2)[None, None, None, :]
    turn = (ky * (2 * half + parity) + 16 * imag) % N
    return wave(turn).reshape(LANES, N // 2)


def wave(turn):
    return (np.cos(2.0 * np.pi * (turn % N) / N) / 8.0).astype(np.float32)


def x_table():
    kx = np.arange(N)[:, None]
    x, imag = np.arange(LANES)[None, :] % N, np.arange(LANES)[None, :] // N
    return np.concatenate([wave(kx * x - 16 * imag), wave(kx * x + 16 * (1 - imag))], axis=1)


def z_table():
    turn = np.arange(N)[:, None] * (np.arange(LANES)[None, :] % N)
    return np.concatenate([wave(turn), wave(turn - 16)], axis=1)


def pair_y_kernel(v_ref, c_ref, e_ref, out_hbm, by_row, by_ky, out_ref, sent):
    v = v_ref[...].astype(f32)
    for i in range(N // 2):
        bands = c_ref[:, i * LANES : (i + 1) * LANES].astype(f32)
        pair = (bands * v[i : i + 1, :]).astype(bf16).astype(f32)
        by_row[pl.ds(i, BANDS, stride=WIDE), :] = pair
    table = e_ref[...]
    low = lane_index((N, LANES)) < N
    half = N // 2
    for j in range(BANDS // 2):
        first = by_row[pl.ds(2 * WIDE * j, half), :]
        second = by_row[pl.ds(2 * WIDE * j + WIDE, half), :]
        both = dot(table, jnp.concatenate([first, second], axis=1).astype(bf16))
        even, odd = both[:N], both[N:]
        even = jnp.where(low, even[:, :LANES], pltpu.roll(even[:, LANES:], N, 1))
        odd = jnp.where(low, pltpu.roll(odd[:, :LANES], N, 1), odd[:, LANES:])
        for start, value in ((2 * j, even + odd), (half * WIDE + 2 * j, even - odd)):
            by_ky[pl.ds(start, half, stride=WIDE), :] = value[:half]
            by_ky[pl.ds(start + 1, half, stride=WIDE), :] = value[half:]
    copies = []
    for place in range(N):
        first, zl = place // 16 * 16 + place % 4, place // 4 % 4
        rows = [by_ky[pl.ds((first + 4 * k) * WIDE + 8 * zl, 8), :] for k in range(4)]
        out_ref[place] = jnp.concatenate(rows, axis=0).astype(bf16)
        if place % 16 == 15:
            part = pl.ds(place - 15, 16)
            copies.append(pltpu.make_async_copy(out_ref.at[part], out_hbm.at[part], sent.at[place // 16]))
            copies[-1].start()
    for copy in copies:
        copy.wait()


def weight_row(fact_ref):
    lane = lane_index((1, LANES))
    chosen = jnp.where(lane.astype(f32) == fact_ref[0:1, :], fact_ref[3:4, :], 0.0)
    filled = jnp.sum(chosen, axis=1, keepdims=True)
    weight = (2.0 * (fact_ref[4:5, :] - filled) / fact_ref[5:6, :])[:, :BANDS]
    band = lax.broadcasted_iota(jnp.int32, (BANDS, LANES), 0).astype(f32)
    pick = jnp.where(band == fact_ref[1:2, :] + (lane % 8).astype(f32), 1.0, 0.0)
    return jnp.dot(weight, pick, precision=lax.Precision.HIGHEST, preferred_element_type=f32)


def spots_kernel(r_ref, e_ref, p_ref, fact_ref, out_ref, planes):
    for x in range(N):
        planes[pl.ds(x * WIDE, 32), :] = r_ref[x].astype(f32)
    column = lane_index((2 * LANES, LANES))
    band = lax.broadcasted_iota(jnp.int32, (2 * LANES, LANES), 0) // N
    total = jnp.zeros((2 * SPOTS, LANES), f32)
    for g in range(4):
        table = jnp.concatenate([e_ref[g, :, :LANES], e_ref[g, :, LANES:]], axis=0)
        cos_z = jnp.concatenate([p_ref[g, :, :LANES].astype(f32)] * 2, axis=1)
        sin_z = jnp.concatenate([p_ref[g, :, LANES:].astype(f32)] * 2, axis=1)
        for h in range(2):
            both = []
            for row in (8 * g + 4 * h, 8 * g + 4 * h + 2):
                parts = [planes[pl.ds(row + k, N, stride=WIDE), :] for k in range(2)]
                both.append(jnp.concatenate(parts, axis=0))
            first, second = both
            at_x = dot(table, jnp.concatenate([first, second], axis=1).astype(bf16))
            real, imag = at_x[:SPOTS], at_x[SPOTS:]
            real_z = real * cos_z + imag * sin_z
            imag_z = imag * cos_z - real * sin_z
            terms = jnp.concatenate([real_z, imag_z], axis=0).astype(bf16)
            ones = jnp.where(column == band + 16 * g + 4 * h, 1.0, 0.0).astype(bf16)
            total = total + dot(terms, ones)
    joined = total[:SPOTS] + pltpu.roll(total[SPOTS:], 8, 1)
    rows = (joined[:ROWS] * weight_row(fact_ref)).T
    for q in range(4):
        cols = joined[ROWS + 16 * q : ROWS + 16 * q + 16]
        cols = cols[:8] + pltpu.roll(cols[8:], N, 1)
        for g in range(4):
            block = [rows[16 * g : 16 * g + 16], cols]
            out_ref[4 * q + g] = jnp.concatenate(block, axis=0).astype(bf16)


def columns_kernel(v_ref, fact_ref, out_ref):
    second = fact_ref[2:3, :] > 0.5
    group = lane_index((32, LANES)) // 16
    rows = [jnp.zeros((32, LANES), f32)] * 4
    for s in range(8):
        core, zl = s // 4, s % 4
        cols = [v_ref[core, 4 * q + zl].astype(f32)[16:] for q in range(4)]
        cols = jnp.concatenate(cols, axis=0)
        cols = jnp.where(second, pltpu.roll(cols, N, 1), cols)
        for g in range(4):
            moved = cols if s == g else pltpu.roll(cols, 16 * (s - g) % LANES, 1)
            rows[g] = jnp.where(group == s, moved, rows[g])
    message = jnp.concatenate(rows, axis=0).astype(bf16)
    for i in range(16):
        out_ref[i] = message


def panel_kernel(a_ref, b_ref, out_hbm, spread, out_ref, sent):
    for y in range(4):
        for x in range(4):
            for zl in range(4):
                at = (16 * y + 4 * zl + x) * WIDE
                spread[pl.ds(at, 32), :] = b_ref[4 * x + y, 32 * zl : 32 * zl + 32, :].astype(f32)
    real_lane = lane_index((ROWS, LANES)) % 16 < 8
    upper, lower = [], []
    for q in range(4):
        rows = [a_ref[s // 4, 4 * q + s % 4].astype(f32)[:16] for s in range(8)]
        rows = jnp.concatenate(rows, axis=0).T
        turned = jnp.where(real_lane, pltpu.roll(rows, LANES - 8, 1), -pltpu.roll(rows, 8, 1))
        upper.append(rows.astype(bf16))
        lower.append(turned.astype(bf16))
    both = jnp.concatenate(
        [jnp.concatenate(upper, axis=1), jnp.concatenate(lower, axis=1)], axis=0
    )
    copies = []
    for h in range(2):
        columns = []
        for j in range(4 * h, 4 * h + 4):
            parts = [spread[pl.ds(8 * q + j, N, stride=WIDE), :] for q in range(4)]
            columns.append(jnp.concatenate(parts, axis=1))
        part = lax.dot_general(
            both,
            jnp.concatenate(columns, axis=0).astype(bf16),
            (((1,), (1,)), ((), ())),
            preferred_element_type=f32,
        )
        part = part * (1.0 / 16.0)
        lanes = pl.ds(h * 256, 256)
        for k in range(2):
            out_ref[k, :, lanes] = part[k * ROWS : (k + 1) * ROWS]
            ends = out_ref.at[k, :, lanes], out_hbm.at[k, :, lanes]
            copies.append(pltpu.make_async_copy(*ends, sent.at[2 * h + k]))
            copies[-1].start()
    for copy in copies:
        copy.wait()


def call(kernel, shape, dtype, scratch, *args, out_space=pltpu.VMEM):
    vmem = pl.BlockSpec(memory_space=pltpu.VMEM)
    return pl.pallas_call(
        kernel,
        out_shape=jax.ShapeDtypeStruct(shape, dtype),
        in_specs=[vmem] * len(args),
        out_specs=pl.BlockSpec(memory_space=out_space),
        scratch_shapes=scratch,
        compiler_params=pltpu.CompilerParams(vmem_limit_bytes=32 * 1024 * 1024),
    )(*args)


def shards(
    valence, conduction, band_index, occ_valence, occ_conduction, gap_energy, row_map, col_map
):
    chosen = band_index[0]
    core = lax.axis_index("c")
    local = lax.all_gather(valence.reshape(-1, N * N), "c", tiled=True)
    band = lax.broadcasted_iota(jnp.int32, local.shape, 0) + local.shape[0] * lax.axis_index("zh")
    own = jnp.sum(jnp.where(band == band_index, local, 0).astype(f32), axis=0)
    v = lax.psum(own.astype(bf16).reshape(32, LANES), "zh")

    half = call(
        pair_y_kernel,
        (N, 32, LANES),
        bf16,
        [
            pltpu.VMEM((BANDS * WIDE, LANES), f32),
            pltpu.VMEM((N * WIDE, LANES), f32),
            pltpu.VMEM((N, 32, LANES), bf16),
            pltpu.SemaphoreType.DMA((4,)),
        ],
        v,
        conduction.reshape(BANDS, N * N),
        jnp.asarray(y_table()).astype(bf16),
        out_space=pl.ANY,
    )
    late = (half, row_map, col_map, occ_valence, occ_conduction, gap_energy)
    late = lax.optimization_barrier(late)
    half, row_map, col_map, occ_valence, occ_conduction, gap_energy = late
    block = lax.all_to_all(half, GA, 0, 0, tiled=True)

    mine = (jnp.arange(4) == lax.axis_index("zl"))[:, None]
    spots = jnp.where(mine, jnp.concatenate([row_map, col_map])[None], 0)
    spots = lax.psum(spots, "zl")
    grid = jnp.arange(N, dtype=jnp.int32)
    table = dot(((spots >> 6)[..., None] == grid).astype(bf16), jnp.asarray(x_table()).astype(bf16))
    phase = dot(((spots & 63)[..., None] == grid).astype(bf16), jnp.asarray(z_table()).astype(bf16))
    facts = [chosen, 8 * lax.axis_index("zl"), core]
    facts = [jnp.full((LANES,), fact) for fact in facts] + [occ_valence, jnp.tile(occ_conduction, 4)]
    facts = jnp.stack([fact.astype(f32) for fact in facts] + [jnp.tile(gap_energy, 4)])
    values = call(
        spots_kernel,
        (16, 24, LANES),
        bf16,
        [pltpu.VMEM((N * WIDE, LANES), f32)],
        block,
        table.astype(bf16),
        phase.astype(bf16),
        facts,
    )

    values = lax.all_to_all(values, ("zh", "zl"), 0, 0, tiled=True)
    values = lax.all_gather(values, "c")
    cols = call(
        columns_kernel,
        (16, ROWS, LANES),
        bf16,
        [],
        values,
        facts,
    )
    columns = lax.all_to_all(cols, ("x", "y"), 0, 0, tiled=True)
    return call(
        panel_kernel,
        (2, ROWS, 8 * N),
        f32,
        [
            pltpu.VMEM((N * WIDE, LANES), f32),
            pltpu.VMEM((2, ROWS, 8 * N), f32),
            pltpu.SemaphoreType.DMA((4,)),
        ],
        values,
        columns,
        out_space=pl.ANY,
    )


def solution(mesh):
    fine = Mesh(mesh.devices.reshape(4, 4, 4, 4, 2), ("y", "zl", "x", "zh", "c"))
    return jax.shard_map(
        shards,
        mesh=fine,
        in_specs=(
            P(COL, GA, None),
            P(COL, GA, None),
            P(),
            P(),
            P(COL),
            P(COL),
            P(GA),
            P(GA),
        ),
        out_specs=P(None, GA, COL),
        check_vma=False,
    )
```

```python
import jax
import jax.numpy as jnp
import numpy as np
from jax import lax
from jax.experimental import pallas as pl
from jax.experimental.pallas import tpu as pltpu
from jax.sharding import Mesh
from jax.sharding import PartitionSpec as P

N = 64
BANDS = 32
ROWS = 128
COLS = 64
SPOTS = ROWS + COLS
LANES = 128
WIDE = 40
GA = ("y", "zl", "x")
COL = ("zh", "c")

f32 = jnp.float32
bf16 = jnp.bfloat16


def dot(left, right):
    return jnp.dot(left, right, preferred_element_type=f32)


def lane_index(shape):
    return lax.broadcasted_iota(jnp.int32, shape, len(shape) - 1)


def y_table():
    parity = np.arange(2)[:, None, None, None]
    imag = np.arange(2)[None, :, None, None]
    ky = np.arange(N // 2)[None, None, :, None]
    half = np.arange(N // 2)[None, None, None, :]
    turn = (ky * (2 * half + parity) + 16 * imag) % N
    return wave(turn).reshape(LANES, N // 2)


def wave(turn):
    return (np.cos(2.0 * np.pi * (turn % N) / N) / 8.0).astype(np.float32)


def x_table():
    kx = np.arange(N)[:, None]
    x, imag = np.arange(LANES)[None, :] % N, np.arange(LANES)[None, :] // N
    return np.concatenate([wave(kx * x - 16 * imag), wave(kx * x + 16 * (1 - imag))], axis=1)


def z_table():
    turn = np.arange(N)[:, None] * (np.arange(LANES)[None, :] % N)
    return np.concatenate([wave(turn), wave(turn - 16)], axis=1)


def pair_y_kernel(v_ref, c_ref, e_ref, out_hbm, by_row, by_ky, out_ref, sent):
    v = v_ref[...].astype(f32)
    for i in range(N // 2):
        bands = c_ref[:, i * LANES : (i + 1) * LANES].astype(f32)
        pair = (bands * v[i : i + 1, :]).astype(bf16).astype(f32)
        by_row[pl.ds(i, BANDS, stride=WIDE), :] = pair
    table = e_ref[...]
    low = lane_index((N, LANES)) < N
    half = N // 2
    for j in range(BANDS // 2):
        first = by_row[pl.ds(2 * WIDE * j, half), :]
        second = by_row[pl.ds(2 * WIDE * j + WIDE, half), :]
        both = dot(table, jnp.concatenate([first, second], axis=1).astype(bf16))
        even, odd = both[:N], both[N:]
        even = jnp.where(low, even[:, :LANES], pltpu.roll(even[:, LANES:], N, 1))
        odd = jnp.where(low, pltpu.roll(odd[:, :LANES], N, 1), odd[:, LANES:])
        for start, value in ((2 * j, even + odd), (half * WIDE + 2 * j, even - odd)):
            by_ky[pl.ds(start, half, stride=WIDE), :] = value[:half]
            by_ky[pl.ds(start + 1, half, stride=WIDE), :] = value[half:]
    copies = []
    for place in range(N):
        first, zl = place // 16 * 16 + place % 4, place // 4 % 4
        rows = [by_ky[pl.ds((first + 4 * k) * WIDE + 8 * zl, 8), :] for k in range(4)]
        out_ref[place] = jnp.concatenate(rows, axis=0).astype(bf16)
        if place % 8 == 7:
            part = pl.ds(place - 7, 8)
            copies.append(pltpu.make_async_copy(out_ref.at[part], out_hbm.at[part], sent.at[place // 8]))
            copies[-1].start()
    for copy in copies:
        copy.wait()


def weight_row(fact_ref):
    lane = lane_index((1, LANES))
    chosen = jnp.where(lane.astype(f32) == fact_ref[0:1, :], fact_ref[3:4, :], 0.0)
    filled = jnp.sum(chosen, axis=1, keepdims=True)
    weight = (2.0 * (fact_ref[4:5, :] - filled) / fact_ref[5:6, :])[:, :BANDS]
    band = lax.broadcasted_iota(jnp.int32, (BANDS, LANES), 0).astype(f32)
    pick = jnp.where(band == fact_ref[1:2, :] + (lane % 8).astype(f32), 1.0, 0.0)
    return jnp.dot(weight, pick, precision=lax.Precision.HIGHEST, preferred_element_type=f32)


def spots_kernel(r_ref, e_ref, p_ref, fact_ref, out_ref, planes):
    for x in range(N):
        planes[pl.ds(x * WIDE, 32), :] = r_ref[x].astype(f32)
    column = lane_index((2 * LANES, LANES))
    band = lax.broadcasted_iota(jnp.int32, (2 * LANES, LANES), 0) // N
    total = jnp.zeros((2 * SPOTS, LANES), f32)
    for g in range(4):
        table = jnp.concatenate([e_ref[g, :, :LANES], e_ref[g, :, LANES:]], axis=0)
        cos_z = jnp.concatenate([p_ref[g, :, :LANES].astype(f32)] * 2, axis=1)
        sin_z = jnp.concatenate([p_ref[g, :, LANES:].astype(f32)] * 2, axis=1)
        for h in range(2):
            both = []
            for row in (8 * g + 4 * h, 8 * g + 4 * h + 2):
                parts = [planes[pl.ds(row + k, N, stride=WIDE), :] for k in range(2)]
                both.append(jnp.concatenate(parts, axis=0))
            first, second = both
            at_x = dot(table, jnp.concatenate([first, second], axis=1).astype(bf16))
            real, imag = at_x[:SPOTS], at_x[SPOTS:]
            real_z = real * cos_z + imag * sin_z
            imag_z = imag * cos_z - real * sin_z
            terms = jnp.concatenate([real_z, imag_z], axis=0).astype(bf16)
            ones = jnp.where(column == band + 16 * g + 4 * h, 1.0, 0.0).astype(bf16)
            total = total + dot(terms, ones)
    joined = total[:SPOTS] + pltpu.roll(total[SPOTS:], 8, 1)
    rows = (joined[:ROWS] * weight_row(fact_ref)).T
    for q in range(4):
        cols = joined[ROWS + 16 * q : ROWS + 16 * q + 16]
        cols = cols[:8] + pltpu.roll(cols[8:], N, 1)
        for g in range(4):
            block = [rows[16 * g : 16 * g + 16], cols]
            out_ref[4 * q + g] = jnp.concatenate(block, axis=0).astype(bf16)


def columns_kernel(v_ref, fact_ref, out_ref):
    second = fact_ref[2:3, :] > 0.5
    group = lane_index((32, LANES)) // 16
    rows = [jnp.zeros((32, LANES), f32)] * 4
    for s in range(8):
        core, zl = s // 4, s % 4
        cols = [v_ref[core, 4 * q + zl].astype(f32)[16:] for q in range(4)]
        cols = jnp.concatenate(cols, axis=0)
        cols = jnp.where(second, pltpu.roll(cols, N, 1), cols)
        for g in range(4):
            moved = cols if s == g else pltpu.roll(cols, 16 * (s - g) % LANES, 1)
            rows[g] = jnp.where(group == s, moved, rows[g])
    message = jnp.concatenate(rows, axis=0).astype(bf16)
    for i in range(16):
        out_ref[i] = message


def panel_kernel(a_ref, b_ref, out_ref, spread):
    for y in range(4):
        for x in range(4):
            for zl in range(4):
                at = (16 * y + 4 * zl + x) * WIDE
                spread[pl.ds(at, 32), :] = b_ref[4 * x + y, 32 * zl : 32 * zl + 32, :].astype(f32)
    real_lane = lane_index((ROWS, LANES)) % 16 < 8
    upper, lower = [], []
    for q in range(4):
        rows = [a_ref[s // 4, 4 * q + s % 4].astype(f32)[:16] for s in range(8)]
        rows = jnp.concatenate(rows, axis=0).T
        turned = jnp.where(real_lane, pltpu.roll(rows, LANES - 8, 1), -pltpu.roll(rows, 8, 1))
        upper.append(rows.astype(bf16))
        lower.append(turned.astype(bf16))
    both = jnp.concatenate(
        [jnp.concatenate(upper, axis=1), jnp.concatenate(lower, axis=1)], axis=0
    )
    for h in range(2):
        columns = []
        for j in range(4 * h, 4 * h + 4):
            parts = [spread[pl.ds(8 * q + j, N, stride=WIDE), :] for q in range(4)]
            columns.append(jnp.concatenate(parts, axis=1))
        part = lax.dot_general(
            both,
            jnp.concatenate(columns, axis=0).astype(bf16),
            (((1,), (1,)), ((), ())),
            preferred_element_type=f32,
        )
        part = part * (1.0 / 16.0)
        out_ref[0, :, h * 256 : (h + 1) * 256] = part[:ROWS]
        out_ref[1, :, h * 256 : (h + 1) * 256] = part[ROWS:]


def call(kernel, shape, dtype, scratch, *args, out_space=pltpu.VMEM):
    vmem = pl.BlockSpec(memory_space=pltpu.VMEM)
    return pl.pallas_call(
        kernel,
        out_shape=jax.ShapeDtypeStruct(shape, dtype),
        in_specs=[vmem] * len(args),
        out_specs=pl.BlockSpec(memory_space=out_space),
        scratch_shapes=scratch,
        compiler_params=pltpu.CompilerParams(vmem_limit_bytes=32 * 1024 * 1024),
    )(*args)


def shards(
    valence, conduction, band_index, occ_valence, occ_conduction, gap_energy, row_map, col_map
):
    chosen = band_index[0]
    core = lax.axis_index("c")
    local = lax.all_gather(valence.reshape(-1, N * N), "c", tiled=True)
    band = lax.broadcasted_iota(jnp.int32, local.shape, 0) + local.shape[0] * lax.axis_index("zh")
    own = jnp.sum(jnp.where(band == band_index, local, 0).astype(f32), axis=0)
    v = lax.psum(own.astype(bf16).reshape(32, LANES), "zh")

    half = call(
        pair_y_kernel,
        (N, 32, LANES),
        bf16,
        [
            pltpu.VMEM((BANDS * WIDE, LANES), f32),
            pltpu.VMEM((N * WIDE, LANES), f32),
            pltpu.VMEM((N, 32, LANES), bf16),
            pltpu.SemaphoreType.DMA((8,)),
        ],
        v,
        conduction.reshape(BANDS, N * N),
        jnp.asarray(y_table()).astype(bf16),
        out_space=pl.ANY,
    )
    late = (half, row_map, col_map, occ_valence, occ_conduction, gap_energy)
    late = lax.optimization_barrier(late)
    half, row_map, col_map, occ_valence, occ_conduction, gap_energy = late
    block = lax.all_to_all(half, GA, 0, 0, tiled=True)

    mine = (jnp.arange(4) == lax.axis_index("zl"))[:, None]
    spots = jnp.where(mine, jnp.concatenate([row_map, col_map])[None], 0)
    spots = lax.psum(spots, "zl")
    grid = jnp.arange(N, dtype=jnp.int32)
    table = dot(((spots >> 6)[..., None] == grid).astype(bf16), jnp.asarray(x_table()).astype(bf16))
    phase = dot(((spots & 63)[..., None] == grid).astype(bf16), jnp.asarray(z_table()).astype(bf16))
    facts = [chosen, 8 * lax.axis_index("zl"), core]
    facts = [jnp.full((LANES,), fact) for fact in facts] + [occ_valence, jnp.tile(occ_conduction, 4)]
    facts = jnp.stack([fact.astype(f32) for fact in facts] + [jnp.tile(gap_energy, 4)])
    values = call(
        spots_kernel,
        (16, 24, LANES),
        bf16,
        [pltpu.VMEM((N * WIDE, LANES), f32)],
        block,
        table.astype(bf16),
        phase.astype(bf16),
        facts,
    )

    values = lax.all_to_all(values, ("zh", "zl"), 0, 0, tiled=True)
    values = lax.all_gather(values, "c")
    cols = call(
        columns_kernel,
        (16, ROWS, LANES),
        bf16,
        [],
        values,
        facts,
    )
    columns = lax.all_to_all(cols, ("x", "y"), 0, 0, tiled=True)
    return call(
        panel_kernel,
        (2, ROWS, 8 * N),
        f32,
        [pltpu.VMEM((N * WIDE, LANES), f32)],
        values,
        columns,
    )


def solution(mesh):
    fine = Mesh(mesh.devices.reshape(4, 4, 4, 4, 2), ("y", "zl", "x", "zh", "c"))
    return jax.shard_map(
        shards,
        mesh=fine,
        in_specs=(
            P(COL, GA, None),
            P(COL, GA, None),
            P(),
            P(),
            P(COL),
            P(COL),
            P(GA),
            P(GA),
        ),
        out_specs=P(None, GA, COL),
        check_vma=False,
    )
```
